512 devices in a mesh: gz: 16 (over x, z_lo), th: 32 (over z_hi, y, core).
Axes of the slice: x: 4, y: 8, z: 8 (z_hi: 2, z_lo: 4; z = z_hi * 4 + z_lo), core: 2. Of those that a mesh axis runs over, the one named last changes fastest.
Arguments:
- density: float32 [256, 64, 2048], P('th', None, 'gz'), may hold values from 0.5 to 2
- velocity: float32 [3, 256, 64, 2048], P(None, 'th', None, 'gz'), may hold values from -3 to 3
- pressure: float32 [256, 64, 2048], P('th', None, 'gz'), may hold values from 0.5 to 2
Outputs:
- advanced: float32 [5, 256, 64, 2048], P(None, 'th', None, 'gz')
The draws below stay inside these ranges and needn't reach their ends.
All inputs are finite; a program needn't handle non-finite values.
Results may differ from the reference program's by a relative error of at most 0.0003.
Values sent between devices are 32-bit elements; how exact they have to be, the bound alone decides.
No kernel may reach another device: no remote copies, remote signals or barrier semaphores. Data moves between devices by JAX's collectives and lax.ppermute only.
A program may use at most 64 MiB of HBM per device.

```python
import math
import jax
import jax.numpy as jnp
from jax import lax

NTH = 256
NR = 64
ZD = 128
NF = 8
NZ = 2048
N_GZ = 16


def block_levels(own_key, shape, pieces, smallest, top_value):
    gain = 1.0
    for position, blocks in pieces:
        steps = jax.random.uniform(jax.random.fold_in(jax.random.fold_in(own_key, 6), position), (blocks,), jnp.float32, smallest / len(pieces), top_value / len(pieces))
        gain = gain * jnp.repeat(jnp.exp(steps), shape[position] // blocks).reshape((-1,) + (1,) * (len(shape) - 1 - position))
    return gain


def gaussian(own_key, extent, spread, most, shards=(), kind=jnp.bfloat16):
    values = jax.random.normal(own_key, extent, jnp.float32) * spread
    if len(shards) > 0:
        values = block_levels(own_key, extent, shards, -0.22, 0.18) * values
    return jnp.clip(values, min=-most, max=most).astype(kind)


def setup_inputs(seed: int = 0) -> dict:
    arg_keys = jax.random.split(jax.random.key(seed), 4)
    density = jnp.clip(jnp.exp(math.log(2.0) - 1.3862944 * jax.random.uniform(arg_keys[0], (NTH, NR, NZ), jnp.float32) ** block_levels(arg_keys[0], (NTH, NR, NZ), ((0, 32), (2, 16)), -0.2, 0.2)), 0.5, 2.0)
    velocity = gaussian(arg_keys[1], (3, NTH, NR, NZ), 0.5, 3.0, ((1, 32), (3, 16)), jnp.float32)
    pressure = jnp.clip(jnp.exp(math.log(2.0) - 1.3862944 * jax.random.uniform(arg_keys[2], (NTH, NR, NZ), jnp.float32) ** block_levels(arg_keys[2], (NTH, NR, NZ), ((0, 32), (2, 16)), -0.2, 0.2)), 0.5, 2.0)
    return {"density": density, "velocity": velocity, "pressure": pressure}


GAMMA_GAS = 1.4
DISSIPATION = 0.2
STEP_FACTOR = 0.25


def conserved(primitive):
    density = primitive[0]
    kinetic = 0.5 * density * (primitive[1] * primitive[1] + primitive[2] * primitive[2] + primitive[3] * primitive[3])
    energy = primitive[4] / (GAMMA_GAS - 1.0) + kinetic
    return jnp.stack([density, density * primitive[1], density * primitive[2], density * primitive[3], energy])


def flux_along(primitive, direction):
    density = primitive[0]
    pressure = primitive[4]
    kinetic = 0.5 * density * (primitive[1] * primitive[1] + primitive[2] * primitive[2] + primitive[3] * primitive[3])
    energy = pressure / (GAMMA_GAS - 1.0) + kinetic
    velocity_along = primitive[1 + direction]
    moving = density * velocity_along
    components = [moving, moving * primitive[1], moving * primitive[2], moving * primitive[3], velocity_along * (energy + pressure)]
    components[1 + direction] = components[1 + direction] + pressure
    return jnp.stack(components)


def tendency(radial_ext, theta_low, theta_high, axial_low, axial_high, radius_ext, theta_step, radial_step):
    radius_mid = radius_ext[:, :, 1:-1, :]
    center = radial_ext[:, :, 1:-1, :]
    conserved_ext = conserved(radial_ext)
    conserved_mid = conserved_ext[:, :, 1:-1, :]
    flux_radial = flux_along(radial_ext, 0) * radius_ext
    div_radial = (flux_radial[:, :, 2:, :] - flux_radial[:, :, :-2, :]) / (2.0 * radial_step * radius_mid)
    div_theta = (flux_along(theta_high, 1) - flux_along(theta_low, 1)) / (2.0 * theta_step * radius_mid)
    div_axial = (flux_along(axial_high, 2) - flux_along(axial_low, 2)) / (2.0 * radial_step)
    smooth_radial = (conserved_ext[:, :, 2:, :] - 2.0 * conserved_mid + conserved_ext[:, :, :-2, :]) / radial_step
    smooth_theta = (conserved(theta_high) - 2.0 * conserved_mid + conserved(theta_low)) / (theta_step * radius_mid)
    smooth_axial = (conserved(axial_high) - 2.0 * conserved_mid + conserved(axial_low)) / radial_step
    smoothing = DISSIPATION * (smooth_radial + smooth_theta + smooth_axial)
    density = center[0]
    radial_speed = center[1]
    azimuth = center[2]
    pressure = center[4]
    zeros_field = jnp.zeros_like(density)
    source = jnp.stack([zeros_field, (density * azimuth * azimuth + pressure) / radius_mid[0],
                        -density * radial_speed * azimuth / radius_mid[0], zeros_field, zeros_field])
    return conserved_mid + (STEP_FACTOR * radial_step) * (smoothing + source - div_radial - div_theta - div_axial)


def wave_tables(points):
    steps_int = jnp.arange(points, dtype=jnp.int32)
    phases = (steps_int[:, None] * steps_int[None, :]) % points
    angles = phases.astype(jnp.float32) * (2.0 * math.pi / points)
    return jnp.cos(angles), jnp.sin(angles)


def filter_gains(cycle_count, points):
    modes = jnp.arange(points, dtype=jnp.int32)
    folded = jnp.minimum(modes, points - modes)
    cycles_int = jnp.arange(cycle_count, dtype=jnp.int32)
    keep = (2 * (cycle_count + 1)) * folded[:, None] <= points * (cycles_int[None, :] + 1)
    return jnp.where(keep, jnp.float32(1.0), jnp.float32(0.0))


def apply_filter(cycle_data, cosine_table, sine_table, damping):
    high = lax.Precision.HIGHEST
    cos_part = jnp.einsum('tm,ftrz->fmrz', cosine_table, cycle_data, precision=high)
    sin_part = jnp.einsum('tm,ftrz->fmrz', sine_table, cycle_data, precision=high)
    weight = damping[None, :, :, None]
    back = jnp.einsum('tm,fmrz->ftrz', cosine_table, cos_part * weight, precision=high)
    back = back + jnp.einsum('tm,fmrz->ftrz', sine_table, sin_part * weight, precision=high)
    return back / cosine_table.shape[0]


def reference(density, velocity, pressure):
    primitive = jnp.concatenate([density[None], velocity, pressure[None]], axis=0)
    extended = jnp.concatenate([primitive[..., -1:], primitive, primitive[..., :1]], axis=3)
    radial_step = 1.0 / NR
    theta_step = 2.0 * math.pi / NTH
    radius_ext = ((jnp.arange(NR + 2, dtype=jnp.float32) - 0.5) * radial_step).reshape(1, 1, NR + 2, 1)
    mirror = jnp.array([1.0, -1.0, -1.0, 1.0, 1.0], dtype=jnp.float32).reshape(5, 1, 1, 1)
    cosine_table, sine_table = wave_tables(NTH)
    damping = filter_gains(NF, NTH)

    def one_slab(block_id):
        window = lax.dynamic_slice_in_dim(extended, (block_id * ZD).astype(jnp.int32), ZD + 2, 3)
        center = window[..., 1:-1]
        partner = jnp.roll(center[:, :, 0:1, :], NTH // 2, axis=1) * mirror
        radial_ext = jnp.concatenate([partner, center, center[:, :, -1:, :]], axis=2)
        updated = tendency(radial_ext, jnp.roll(center, 1, axis=1), jnp.roll(center, -1, axis=1),
                           window[..., :-2], window[..., 2:], radius_ext, theta_step, radial_step)
        filtered = apply_filter(updated[:, :, :NF, :], cosine_table, sine_table, damping)
        return jnp.concatenate([filtered, updated[:, :, NF:, :]], axis=2)

    blocks = lax.map(one_slab, jnp.arange(N_GZ, dtype=jnp.int32))
    return jnp.moveaxis(blocks, 0, 3).reshape(5, NTH, NR, NZ)
```

```python
import math

import jax
import jax.numpy as jnp
import ml_dtypes
import numpy as np
from jax import lax
from jax.experimental import pallas as pl
from jax.experimental.pallas import tpu as pltpu
from jax.sharding import PartitionSpec as P

NTH = 256
NR = 64
NF = 8
N_TH = 32
SECTOR = NTH // N_TH
LANES = 128
FIELDS = 5
SEND_ROWS = 16
BACK_ROWS = 18

HALF_STEP = 0.125
SMOOTH = 0.05


def theta_factor(cycle):
    return 0.25 / (2.0 * (2.0 * math.pi / NTH) * (cycle + 0.5))


def filter_rows():
    modes = np.arange(NTH)
    folded = np.minimum(modes, NTH - modes)
    waves = np.cos(2.0 * math.pi * (modes[:, None] * modes[None, :] % NTH) / NTH)
    rows = []
    for cycle in range(NF):
        keep = 2 * (NF + 1) * folded <= NTH * (cycle + 1)
        rows.append(waves[:, keep].sum(axis=1) / NTH)
    return np.stack(rows)


def filter_matrices():
    rows = filter_rows()
    index = (np.arange(NTH)[:, None] - np.arange(NTH)[None, :]) % NTH
    full = np.concatenate([rows[:, index], rows[:1, (index + NTH // 2) % NTH]]).astype(np.float32)
    high = full.astype(ml_dtypes.bfloat16)
    low = (full - high.astype(np.float32)).astype(ml_dtypes.bfloat16)
    return high, low


def edge_weights():
    rows = filter_rows()
    table = np.zeros((2 * N_TH, SECTOR, LANES), np.float32)
    for row in range(2 * N_TH - 1):
        apart = (N_TH - 1 - row) * SECTOR
        index = (apart + np.arange(SECTOR)[:, None] - np.arange(SECTOR)[None, :]) % NTH
        block = np.repeat(rows[:, index].transpose(1, 0, 2)[..., None], 2, axis=3)
        table[row] = block.reshape(SECTOR, LANES)
    return table


def conserved(fields):
    rho, ur, ut, uz, p = fields
    qr, qt, qz = rho * ur, rho * ut, rho * uz
    energy = p * 2.5 + 0.5 * (qr * ur + qt * ut + qz * uz)
    return rho, qr, qt, qz, energy


def flux(fields, q, direction):
    p = fields[4]
    speed = fields[1 + direction]
    moving = q[1 + direction]
    parts = [moving, moving * fields[1], moving * fields[2], moving * fields[3], speed * (q[4] + p)]
    parts[1 + direction] = parts[1 + direction] + p
    return parts


def lanes_of(shape):
    return lax.broadcasted_iota(jnp.int32, shape, len(shape) - 1)


def rows_of(shape):
    return lax.broadcasted_iota(jnp.int32, shape, len(shape) - 2)


def spread(value, shift, axis):
    size = value.shape[axis]
    return pltpu.roll(value, shift % size, axis)


def half_packs(tile):
    turned = spread(tile, 64, 1)
    low = lanes_of((SECTOR, LANES)) < 64
    first = jnp.where(low, tile, spread(turned, 4, 0))
    second = jnp.where(low, turned, spread(tile, 4, 0))
    return first[:4], second[:4]


def inner_kernel(d_ref, v_ref, p_ref, out_ref):
    def load(cycle):
        return (
            d_ref[:, cycle, :],
            v_ref[0, :, cycle, :],
            v_ref[1, :, cycle, :],
            v_ref[2, :, cycle, :],
            p_ref[:, cycle, :],
        )

    shape = (SECTOR, LANES)
    lane, row = lanes_of(shape), rows_of(shape)
    not_first_lane, not_last_lane = lane > 0, lane < LANES - 1
    not_first_row, not_last_row = row > 0, row < SECTOR - 1
    out_ref[...] = jnp.zeros(out_ref.shape, jnp.float32)

    before = None
    fields = load(0)
    q = conserved(fields)
    radial = flux(fields, q, 0)
    for f in range(FIELDS):
        sign = -1.0 if f in (1, 2) else 1.0
        mirrored = sign * (SMOOTH * q[f] + HALF_STEP * radial[f])
        for half, pack in enumerate(half_packs(mirrored)):
            out_ref[16 + 2 * f + half, 10:14, :] = pack
    for cycle in range(NF):
        after_fields = load(cycle + 1)
        after_q = conserved(after_fields)
        after = (after_q, flux(after_fields, after_q, 0))
        around = flux(fields, q, 1)
        along = flux(fields, q, 2)
        c = theta_factor(cycle)
        radius = cycle + 0.5
        scale = 0.25 / radius
        sources = (
            None,
            scale * (q[2] * fields[2] + fields[4]),
            -scale * (q[1] * fields[2]),
            None,
            None,
        )
        for f in range(FIELDS):
            own = q[f] * (0.8 - 0.8 * c)
            if sources[f] is not None:
                own = own + sources[f]
            smooth, push = SMOOTH * q[f], HALF_STEP * along[f]
            own = own + jnp.where(not_first_lane, spread(smooth + push, 1, 1), 0.0)
            own = own + jnp.where(not_last_lane, spread(smooth - push, -1, 1), 0.0)
            smooth, push = (0.4 * c) * q[f], c * around[f]
            rising, falling = smooth + push, smooth - push
            own = own + jnp.where(not_first_row, spread(rising, 1, 0), 0.0)
            own = own + jnp.where(not_last_row, spread(falling, -1, 0), 0.0)
            own = own + (SMOOTH * after[0][f] - (HALF_STEP * (radius + 1.0) / radius) * after[1][f])
            if before is not None:
                own = own + (SMOOTH * before[0][f] + (HALF_STEP * (radius - 1.0) / radius) * before[1][f])
            if f < 4:
                unit = f * NF + cycle
                out_ref[unit, 0:8, :] = own
                out_ref[unit, 8:9, :] = rising[7:8]
                out_ref[unit, 15:16, :] = falling[0:1]
            else:
                packs = half_packs(own)
                up, down = rising[7:8], falling[0:1]
                up_turned, down_turned = spread(up, 64, 1), spread(down, 64, 1)
                for half in range(2):
                    unit = half * NF + cycle
                    out_ref[unit, 10:14, :] = packs[half]
                    out_ref[unit, 9:10, :] = down if half == 0 else down_turned
                    out_ref[unit, 14:15, :] = up_turned if half == 0 else up
        before = (q, radial)
        fields, q, radial = after_fields, after_q, after[1]


def inner_part(density, velocity, pressure):
    return pl.pallas_call(
        inner_kernel,
        grid=(1,),
        in_specs=[
            pl.BlockSpec((SECTOR, 16, LANES), lambda i: (0, 0, 0)),
            pl.BlockSpec((3, SECTOR, 16, LANES), lambda i: (0, 0, 0, 0)),
            pl.BlockSpec((SECTOR, 16, LANES), lambda i: (0, 0, 0)),
        ],
        out_specs=pl.BlockSpec((N_TH, SEND_ROWS, LANES), lambda i: (0, 0, 0)),
        out_shape=jax.ShapeDtypeStruct((N_TH, SEND_ROWS, LANES), jnp.float32),
        cost_estimate=pl.CostEstimate(flops=8 * 1024 * 200, bytes_accessed=600_000, transcendentals=0),
        name="inner_part",
    )(density, velocity, pressure)


def edge_kernel(odd_ref, d_ref, v_ref, p_ref, columns_ref, near_ref, far_ref):
    lane = lanes_of((NR, LANES))
    odd = odd_ref[0] == 1

    def load(f, j):
        return d_ref[j] if f == 0 else (p_ref[j] if f == 4 else v_ref[f - 1, j])

    total = jnp.zeros((NR, LANES), jnp.float32)
    for f in range(FIELDS):
        for j in range(SECTOR):
            spot = 16 * f + 2 * j + 1
            total = jnp.where((lane == spot) | (lane == spot + 1), spread(load(f, j), spot + 1, 1), total)
        first, last = load(f, 0), load(f, SECTOR - 1)
        near_ref[f] = jnp.where(odd, first, last)
        far_ref[f] = jnp.where(odd, last, first)
    columns_ref[...] = total


def edges(odd, density, velocity, pressure):
    vmem = pl.BlockSpec(memory_space=pltpu.VMEM)
    rows = jax.ShapeDtypeStruct((FIELDS, NR, LANES), jnp.float32)
    return pl.pallas_call(
        edge_kernel,
        in_specs=[pl.BlockSpec(memory_space=pltpu.SMEM), vmem, vmem, vmem],
        out_specs=[vmem, vmem, vmem],
        out_shape=[jax.ShapeDtypeStruct((NR, LANES), jnp.float32), rows, rows],
        cost_estimate=pl.CostEstimate(flops=320 * 1024 * 3, bytes_accessed=1_800_000, transcendentals=0),
        name="edges",
    )(odd, density, velocity, pressure)


def axial_terms(near, far, odd):
    lane = lanes_of(near.shape)
    before = jnp.where(odd, near, far)
    after = jnp.where(odd, far, near)
    both = jnp.where(lane % 2 == 1, before, spread(after, -2, 1))
    fields = [both] + [spread(both, -16 * f, 1) for f in range(1, FIELDS)]
    q = conserved(fields)
    along = flux(fields, q, 2)
    push = jnp.where(lane % 2 == 1, HALF_STEP, -HALF_STEP)
    return [SMOOTH * q[f] + push * along[f] for f in range(FIELDS)]


def filter_kernel(which_ref, odd_ref, r_ref, wh_ref, wl_ref, hh_ref, hl_ref, near_ref, far_ref, out_ref):
    del which_ref
    shape = (N_TH, SECTOR, LANES)
    row, lane = rows_of(shape), lanes_of(shape)
    main = r_ref[:, 0:8, :]
    extra = r_ref[:, 8:16, :]
    before = jnp.concatenate([extra[-1:], extra[:-1]], axis=0)
    after = jnp.concatenate([extra[1:], extra[:1]], axis=0)
    zero = jnp.zeros(shape, jnp.float32)
    main = main + jnp.where(row == 0, before, jnp.where(row == 7, after, zero))
    turned = spread(extra, 64, 2)
    top = spread(extra, 6, 1)
    bottom = spread(turned, 2, 1)
    half = jnp.where(row < 4, top, bottom)
    half = half + jnp.where(
        row == 0,
        jnp.concatenate([bottom[-1:], bottom[:-1]], axis=0),
        jnp.where(row == 7, jnp.concatenate([top[1:], top[:1]], axis=0), zero),
    )

    def product(high, low, value):
        value = value.reshape(NTH, LANES)
        big = value.astype(jnp.bfloat16)
        small = (value - big.astype(jnp.float32)).astype(jnp.bfloat16)
        out = jnp.dot(high, big, preferred_element_type=jnp.float32)
        out = out + jnp.dot(high, small, preferred_element_type=jnp.float32)
        out = out + jnp.dot(low, big, preferred_element_type=jnp.float32)
        return out.reshape(shape)

    main = product(wh_ref[0], wl_ref[0], main)
    half = product(hh_ref[0], hl_ref[0], half)
    packed = jnp.where(lane < 64, half, spread(spread(half, 64, 2), 4, 1))

    terms = axial_terms(near_ref[...], far_ref[...], odd_ref[1] == 1)
    first = lanes_of((NF, LANES)) < 16
    border = [
        jnp.sum(
            pltpu.roll(jnp.where(first, term, 0.0), 0, 1, stride=16, stride_axis=0), axis=0, keepdims=True
        )
        for term in terms
    ]
    border = jnp.concatenate(border + [jnp.zeros((1, LANES), jnp.float32)], axis=0)
    for s in range(N_TH):
        base = s * BACK_ROWS
        out_ref[base : base + 8, :] = main[s]
        out_ref[base + 8 : base + 12, :] = packed[s, :4]
        out_ref[base + 12 : base + 18, :] = border


def filtered(which, odd, received, high, low, near, far):
    matrix = (1, NTH, NTH)
    grid_spec = pltpu.PrefetchScalarGridSpec(
        num_scalar_prefetch=2,
        grid=(1,),
        in_specs=[
            pl.BlockSpec((N_TH, SEND_ROWS, LANES), lambda i, w, o: (0, 0, 0)),
            pl.BlockSpec(matrix, lambda i, w, o: (w[0], 0, 0)),
            pl.BlockSpec(matrix, lambda i, w, o: (w[0], 0, 0)),
            pl.BlockSpec(matrix, lambda i, w, o: (w[1], 0, 0)),
            pl.BlockSpec(matrix, lambda i, w, o: (w[1], 0, 0)),
            pl.BlockSpec((NF, LANES), lambda i, w, o: (0, 0)),
            pl.BlockSpec((NF, LANES), lambda i, w, o: (0, 0)),
        ],
        out_specs=pl.BlockSpec((N_TH * BACK_ROWS, LANES), lambda i, w, o: (0, 0)),
    )
    return pl.pallas_call(
        filter_kernel,
        grid_spec=grid_spec,
        out_shape=jax.ShapeDtypeStruct((N_TH * BACK_ROWS, LANES), jnp.float32),
        cost_estimate=pl.CostEstimate(flops=6 * 256 * 256 * 256, bytes_accessed=1_200_000, transcendentals=0),
        name="filtered",
    )(which, odd, received, high, low, high, low, near, far)


def outer_kernel(odd_ref, d_ref, v_ref, p_ref, side_ref, back_ref, near_ref, far_ref, out_ref, terms_ref):
    th_odd, gz_odd = odd_ref[0] == 1, odd_ref[1] == 1
    terms = axial_terms(near_ref[...], far_ref[...], gz_odd)
    for f in range(FIELDS):
        terms_ref[f] = terms[f]
    shape = (NR, LANES)
    lane, row = lanes_of(shape), rows_of(shape)
    radius = row.astype(jnp.float32) + 0.5
    inverse = 1.0 / radius
    c = theta_factor(0) * 0.5 * inverse

    def load(j):
        return (d_ref[j], v_ref[0, j], v_ref[1, j], v_ref[2, j], p_ref[j])

    def step(j, carry):
        fields = load(j)
        below = load(jnp.maximum(j - 1, 0))
        above = load(jnp.minimum(j + 1, SECTOR - 1))
        use_low, use_high = j == 0, j == SECTOR - 1
        below = [
            jnp.where(use_low, jnp.where(th_odd, side_ref[f], back_ref[f]), below[f]) for f in range(FIELDS)
        ]
        above = [
            jnp.where(use_high, jnp.where(th_odd, back_ref[f], side_ref[f]), above[f]) for f in range(FIELDS)
        ]
        q = conserved(fields)
        radial = flux(fields, q, 0)
        along = flux(fields, q, 2)
        q_low, q_high = conserved(below), conserved(above)
        f_low, f_high = flux(below, q_low, 1), flux(above, q_high, 1)
        scale = 0.25 * inverse
        sources = (
            None,
            scale * (q[2] * fields[2] + fields[4]),
            -scale * (q[1] * fields[2]),
            None,
            None,
        )
        for f in range(FIELDS):
            own = q[f] * (0.8 - 0.8 * c)
            if sources[f] is not None:
                own = own + sources[f]
            smooth, push = SMOOTH * q[f], HALF_STEP * along[f]
            side = spread(terms_ref[f], LANES - 1 - 2 * j, 1)
            own = own + jnp.where(lane == 0, side, spread(smooth + push, 1, 1))
            own = own + jnp.where(lane == LANES - 1, side, spread(smooth - push, LANES - 1, 1))
            own = own + c * (0.4 * (q_low[f] + q_high[f]) + (f_low[f] - f_high[f]))
            push = (HALF_STEP * radius) * radial[f]
            smooth_ahead = jnp.where(row == NR - 1, smooth, spread(smooth, NR - 1, 0))
            push_ahead = jnp.where(row == NR - 1, push + HALF_STEP * radial[f], spread(push, NR - 1, 0))
            own = own + (smooth_ahead + spread(smooth, 1, 0))
            own = own + inverse * (spread(push, 1, 0) - push_ahead)
            out_ref[f, j] = own
        return carry

    lax.fori_loop(0, SECTOR, step, 0)


def outer_part(odd, density, velocity, pressure, side, back, near, far, token):
    vmem = pl.BlockSpec(memory_space=pltpu.VMEM)

    def kernel(odd_ref, d, v, p, s, b, n, f, token_ref, out_ref, terms_ref):
        del token_ref
        outer_kernel(odd_ref, d, v, p, s, b, n, f, out_ref, terms_ref)

    return pl.pallas_call(
        kernel,
        in_specs=[pl.BlockSpec(memory_space=pltpu.SMEM)] + [vmem] * 7 + [pl.BlockSpec(memory_space=pl.ANY)],
        out_specs=vmem,
        out_shape=jax.ShapeDtypeStruct((FIELDS, SECTOR, NR, LANES), jnp.float32),
        scratch_shapes=[pltpu.VMEM((FIELDS, NR, LANES), jnp.float32)],
        cost_estimate=pl.CostEstimate(flops=64 * 1024 * 250, bytes_accessed=3_000_000, transcendentals=0),
        name="outer_part",
    )(odd, density, velocity, pressure, side, back, near, far, token)


def finish_kernel(place_ref, r_ref, w_ref, rest_ref, out_ref):
    del rest_ref
    start = N_TH - 1 - place_ref[0]
    shape = (SECTOR, LANES)
    lane = lanes_of(shape)
    low_half = lanes_of((4, LANES)) < 64
    ends = (lane == 0) | (lane == LANES - 1)

    sums = [jnp.zeros(shape, jnp.float32) for _ in range(FIELDS)]
    for t in range(N_TH):
        weights = w_ref[start + t]
        base = t * BACK_ROWS + 12
        for f in range(FIELDS):
            sums[f] = sums[f] + weights * r_ref[base + f : base + f + 1, :]
    for f in range(FIELDS):
        for shift in (2, 4, 8):
            sums[f] = sums[f] + spread(sums[f], -shift, 1)

    def joined(unit_a, unit_b):
        a = r_ref[unit_a * BACK_ROWS + 8 : unit_a * BACK_ROWS + 12, :]
        b = r_ref[unit_b * BACK_ROWS + 8 : unit_b * BACK_ROWS + 12, :]
        top = jnp.where(low_half, a, spread(b, 64, 1))
        bottom = jnp.where(low_half, spread(a, 64, 1), b)
        return jnp.concatenate([top, bottom], axis=0)

    for f in range(FIELDS):
        for cycle in range(NF):
            if f < 4:
                unit = (f * NF + cycle) * BACK_ROWS
                tile = r_ref[unit : unit + 8, :]
            else:
                tile = joined(cycle, NF + cycle)
            if cycle == 0:
                tile = tile + joined(16 + 2 * f, 17 + 2 * f)
            tile = tile + jnp.where(ends, spread(sums[f], -(16 * cycle + 1), 1), 0.0)
            out_ref[f, :, cycle, :] = tile


def finish(place, received, weights, rest):
    inner = pl.BlockSpec((FIELDS, SECTOR, NF, LANES), lambda i, p: (0, 0, 0, 0))
    grid_spec = pltpu.PrefetchScalarGridSpec(
        num_scalar_prefetch=1,
        grid=(1,),
        in_specs=[
            pl.BlockSpec((N_TH * BACK_ROWS, LANES), lambda i, p: (0, 0)),
            pl.BlockSpec((2 * N_TH, SECTOR, LANES), lambda i, p: (0, 0, 0)),
            pl.BlockSpec(memory_space=pl.ANY),
        ],
        out_specs=inner,
    )
    return pl.pallas_call(
        finish_kernel,
        grid_spec=grid_spec,
        out_shape=jax.ShapeDtypeStruct((FIELDS, SECTOR, NR, LANES), jnp.float32),
        input_output_aliases={3: 0},
        cost_estimate=pl.CostEstimate(flops=400 * 1024, bytes_accessed=800_000, transcendentals=0),
        name="finish",
    )(place, received, weights, rest)


def pairs(size, offset):
    return [(i, (((i - offset) ^ 1) + offset) % size) for i in range(size)]


def per_device(density, velocity, pressure):
    high, low = filter_matrices()
    high, low = jnp.asarray(high), jnp.asarray(low)
    weights = jnp.asarray(edge_weights())
    th, gz = lax.axis_index("th"), lax.axis_index("gz")
    odd = jnp.stack([th % 2, gz % 2]).astype(jnp.int32)
    main = th % NF
    half = jnp.where(th < 16, main, jnp.where(th < 26, NF, 0))
    which = jnp.stack([main, half]).astype(jnp.int32)
    place = th.astype(jnp.int32).reshape(1)

    sent = inner_part(density, velocity, pressure)
    received = lax.all_to_all(sent, "th", 0, 0, tiled=True)

    columns, near_row, far_row = edges(odd, density, velocity, pressure)
    gz_near = lax.ppermute(columns, "gz", pairs(lax.axis_size("gz"), 0))
    gz_far = lax.ppermute(columns, "gz", pairs(lax.axis_size("gz"), 1))
    th_near = lax.ppermute(near_row, "th", pairs(N_TH, 0))
    th_far = lax.ppermute(far_row, "th", pairs(N_TH, 1))

    back = filtered(which, odd, received, high, low, gz_near, gz_far)
    returned = lax.all_to_all(
        back.reshape(N_TH, BACK_ROWS // 2, 2, LANES), "th", 0, 0, tiled=True
    ).reshape(N_TH * BACK_ROWS, LANES)
    rest = outer_part(odd, density, velocity, pressure, th_near, th_far, gz_near, gz_far, back)
    return finish(place, returned, weights, rest)


def solution(mesh):
    in_specs = (P("th", None, "gz"), P(None, "th", None, "gz"), P("th", None, "gz"))
    out_specs = P(None, "th", None, "gz")
    return jax.shard_map(
        per_device, mesh=mesh, in_specs=in_specs, out_specs=out_specs, check_vma=False
    )
```

```python
import math

import jax
import jax.numpy as jnp
import ml_dtypes
import numpy as np
from jax import lax
from jax.experimental import pallas as pl
from jax.experimental.pallas import tpu as pltpu
from jax.sharding import PartitionSpec as P

NTH = 256
NR = 64
NF = 8
N_TH = 32
SECTOR = NTH // N_TH
LANES = 128
FIELDS = 5
SEND_ROWS = 20
BACK_ROWS = 12
SHARE = N_TH * FIELDS

HALF_STEP = 0.125
SMOOTH = 0.05


def theta_factor(cycle):
    return 0.25 / (2.0 * (2.0 * math.pi / NTH) * (cycle + 0.5))


def filter_rows():
    modes = np.arange(NTH)
    folded = np.minimum(modes, NTH - modes)
    waves = np.cos(2.0 * math.pi * (modes[:, None] * modes[None, :] % NTH) / NTH)
    rows = []
    for cycle in range(NF):
        keep = 2 * (NF + 1) * folded <= NTH * (cycle + 1)
        rows.append(waves[:, keep].sum(axis=1) / NTH)
    return np.stack(rows)


def filter_matrices():
    rows = filter_rows()
    index = (np.arange(NTH)[:, None] - np.arange(NTH)[None, :]) % NTH
    full = np.concatenate([rows[:, index], rows[:1, (index + NTH // 2) % NTH]]).astype(np.float32)
    high = full.astype(ml_dtypes.bfloat16)
    low = (full - high.astype(np.float32)).astype(ml_dtypes.bfloat16)
    return high, low


def edge_weights():
    rows = filter_rows()
    table = np.zeros((2 * N_TH, SECTOR, LANES), np.float32)
    for row in range(2 * N_TH - 1):
        apart = (N_TH - 1 - row) * SECTOR
        index = (apart + np.arange(SECTOR)[:, None] - np.arange(SECTOR)[None, :]) % NTH
        block = np.repeat(rows[:, index].transpose(1, 0, 2)[..., None], 2, axis=3)
        table[row] = block.reshape(SECTOR, LANES)
    return table


def conserved(fields):
    rho, ur, ut, uz, p = fields
    qr, qt, qz = rho * ur, rho * ut, rho * uz
    energy = p * 2.5 + 0.5 * (qr * ur + qt * ut + qz * uz)
    return rho, qr, qt, qz, energy


def flux(fields, q, direction):
    p = fields[4]
    speed = fields[1 + direction]
    moving = q[1 + direction]
    parts = [moving, moving * fields[1], moving * fields[2], moving * fields[3], speed * (q[4] + p)]
    parts[1 + direction] = parts[1 + direction] + p
    return parts


def lanes_of(shape):
    return lax.broadcasted_iota(jnp.int32, shape, len(shape) - 1)


def rows_of(shape):
    return lax.broadcasted_iota(jnp.int32, shape, len(shape) - 2)


def spread(value, shift, axis):
    size = value.shape[axis]
    return pltpu.roll(value, shift % size, axis)


def half_packs(tile):
    turned = spread(tile, 64, 1)
    low = lanes_of((SECTOR, LANES)) < 64
    first = jnp.where(low, tile, spread(turned, 4, 0))
    second = jnp.where(low, turned, spread(tile, 4, 0))
    return first[:4], second[:4]


def inner_kernel(d_ref, v_ref, p_ref, out_ref):
    def load(cycle):
        return (
            d_ref[:, cycle, :],
            v_ref[0, :, cycle, :],
            v_ref[1, :, cycle, :],
            v_ref[2, :, cycle, :],
            p_ref[:, cycle, :],
        )

    def store(unit, row, value):
        start = unit * SEND_ROWS + row
        out_ref[start : start + value.shape[0], :] = value

    shape = (SECTOR, LANES)
    lane, row = lanes_of(shape), rows_of(shape)
    first_lane, last_lane = lane == 0, lane == LANES - 1
    not_first_row, not_last_row = row > 0, row < SECTOR - 1
    low = lanes_of((1, LANES)) < 64
    for unit in range(16, N_TH):
        store(unit, 9, jnp.zeros((5, LANES), jnp.float32))

    before = None
    fields = load(0)
    q = conserved(fields)
    radial = flux(fields, q, 0)
    for f in range(FIELDS):
        sign = -1.0 if f in (1, 2) else 1.0
        mirrored = sign * (SMOOTH * q[f] + HALF_STEP * radial[f])
        for half, pack in enumerate(half_packs(mirrored)):
            store(16 + 2 * f + half, 10, pack)
    border = [jnp.zeros(shape, jnp.float32) for _ in range(FIELDS)]
    for cycle in range(NF):
        after_fields = load(cycle + 1)
        after_q = conserved(after_fields)
        after = (after_q, flux(after_fields, after_q, 0))
        around = flux(fields, q, 1)
        along = flux(fields, q, 2)
        c = theta_factor(cycle)
        radius = cycle + 0.5
        scale = 0.25 / radius
        sources = (
            None,
            scale * (q[2] * fields[2] + fields[4]),
            -scale * (q[1] * fields[2]),
            None,
            None,
        )
        for f in range(FIELDS):
            own = q[f] * (0.8 - 0.8 * c)
            if sources[f] is not None:
                own = own + sources[f]
            smooth, push = SMOOTH * q[f], HALF_STEP * along[f]
            forward, backward = spread(smooth + push, 1, 1), spread(smooth - push, -1, 1)
            own = own + jnp.where(first_lane, 0.0, forward) + jnp.where(last_lane, 0.0, backward)
            beyond = jnp.where(first_lane, forward, jnp.where(last_lane, backward, 0.0))
            border[f] = border[f] + spread(beyond, 16 * cycle + 1, 1)
            smooth, push = (0.4 * c) * q[f], c * around[f]
            rising, falling = smooth + push, smooth - push
            own = own + jnp.where(not_first_row, spread(rising, 1, 0), 0.0)
            own = own + jnp.where(not_last_row, spread(falling, -1, 0), 0.0)
            own = own + (SMOOTH * after[0][f] - (HALF_STEP * (radius + 1.0) / radius) * after[1][f])
            if before is not None:
                own = own + (SMOOTH * before[0][f] + (HALF_STEP * (radius - 1.0) / radius) * before[1][f])
            up, down = rising[7:8], falling[0:1]
            if f < 4:
                unit = f * NF + cycle
                store(unit, 0, own)
                store(unit, 8, up)
                store(unit, 15, down)
            else:
                packs = half_packs(own)
                store(cycle, 10, packs[0])
                store(cycle, 9, jnp.where(low, down, spread(up, 64, 1)))
                store(NF + cycle, 10, packs[1])
                store(NF + cycle, 9, jnp.where(low, spread(down, 64, 1), up))
        before = (q, radial)
        fields, q, radial = after_fields, after_q, after[1]
    rows = [
        jnp.sum(pltpu.roll(value, 0, 1, stride=2, stride_axis=0), axis=0, keepdims=True) for value in border
    ]
    others = jnp.concatenate(rows[1:], axis=0)
    for unit in range(N_TH):
        store(unit, 14, rows[0])
        store(unit, 16, others)


def in_vmem(value):
    return pltpu.with_memory_space_constraint(value, pltpu.VMEM)


def in_hbm(value):
    return pltpu.with_memory_space_constraint(value, pltpu.HBM)


PARAMS = pltpu.CompilerParams(vmem_limit_bytes=24 << 20)
WHOLE = pl.BlockSpec(memory_space=pltpu.VMEM)
SCALARS = pl.BlockSpec(memory_space=pltpu.SMEM)


def inner_part(density, velocity, pressure):
    return pl.pallas_call(
        inner_kernel,
        grid=(1,),
        in_specs=[
            pl.BlockSpec((SECTOR, 16, LANES), lambda i: (0, 0, 0)),
            pl.BlockSpec((3, SECTOR, 16, LANES), lambda i: (0, 0, 0, 0)),
            pl.BlockSpec((SECTOR, 16, LANES), lambda i: (0, 0, 0)),
        ],
        out_specs=WHOLE,
        out_shape=pltpu.VMEM((N_TH * SEND_ROWS, LANES), jnp.float32),
        compiler_params=PARAMS,
        cost_estimate=pl.CostEstimate(flops=8 * 1024 * 200, bytes_accessed=600_000, transcendentals=0),
        name="inner_part",
    )(in_hbm(density), in_hbm(velocity), in_hbm(pressure))


def edge_kernel(odd_ref, high_ref, low_ref, d_ref, v_ref, p_ref, near_ref, far_ref, columns_ref, w_ref, done):
    copies = [
        pltpu.make_async_copy(table.at[odd_ref[1 + k]], w_ref.at[2 * k + n], done.at[2 * k + n])
        for k in range(2)
        for n, table in enumerate((high_ref, low_ref))
    ]
    for copy in copies:
        copy.start()
    lane = lanes_of((NR, LANES))
    odd = odd_ref[0] == 1

    def load(f, j):
        return d_ref[j] if f == 0 else (p_ref[j] if f == 4 else v_ref[f - 1, j])

    total = jnp.zeros((NR, LANES), jnp.float32)
    for f in range(FIELDS):
        for j in range(SECTOR):
            spot = 16 * f + 2 * j + 1
            total = jnp.where((lane == spot) | (lane == spot + 1), spread(load(f, j), spot + 1, 1), total)
        first, last = load(f, 0), load(f, SECTOR - 1)
        near_ref[f] = jnp.where(odd, first, last)
        far_ref[f] = jnp.where(odd, last, first)
    columns_ref[...] = total
    for copy in copies:
        copy.wait()


def edges(which, high, low, density, velocity, pressure):
    rows = pltpu.VMEM((FIELDS, NR, LANES), jnp.float32)
    return pl.pallas_call(
        edge_kernel,
        in_specs=[SCALARS] + [pl.BlockSpec(memory_space=pl.ANY)] * 2 + [WHOLE] * 3,
        out_specs=[WHOLE] * 4,
        out_shape=[
            rows,
            rows,
            pltpu.VMEM((NR, LANES), jnp.float32),
            pltpu.VMEM((4, NTH, NTH), jnp.bfloat16),
        ],
        scratch_shapes=[pltpu.SemaphoreType.DMA((4,))],
        compiler_params=PARAMS,
        cost_estimate=pl.CostEstimate(flops=320 * 1024 * 3, bytes_accessed=1_800_000, transcendentals=0),
        name="edges",
    )(which, in_hbm(high), in_hbm(low), in_vmem(density), in_vmem(velocity), in_vmem(pressure))


def axial_terms(before, after):
    lane = lanes_of(before.shape)
    both = jnp.where(lane % 2 == 1, before, spread(after, -2, 1))
    fields = [both] + [spread(both, -16 * f, 1) for f in range(1, FIELDS)]
    q = conserved(fields)
    along = flux(fields, q, 2)
    push = jnp.where(lane % 2 == 1, HALF_STEP, -HALF_STEP)
    return [SMOOTH * q[f] + push * along[f] for f in range(FIELDS)]


def filter_kernel(r_ref, w_ref, columns_ref, out_ref, share_ref):
    shape = (N_TH, SECTOR, LANES)
    row, lane = rows_of(shape), lanes_of(shape)
    starts = [s * SEND_ROWS for s in range(N_TH)]
    main = jnp.stack([r_ref[a : a + 8, :] for a in starts])
    extra = jnp.stack([r_ref[a + 8 : a + 16, :] for a in starts])
    zero = jnp.zeros(shape, jnp.float32)

    def earlier(value):
        return jnp.concatenate([value[-1:], value[:-1]], axis=0)

    def later(value):
        return jnp.concatenate([value[1:], value[:1]], axis=0)

    main = main + jnp.where(row == 0, earlier(extra), jnp.where(row == 7, later(extra), zero))
    turned = spread(extra, 64, 2)
    top = spread(extra, 6, 1)
    half = jnp.where(row < 4, top, spread(turned, 2, 1))
    half = half + jnp.where(
        row == 0, earlier(spread(turned, 7, 1)), jnp.where(row == 7, later(top), zero)
    )

    def product(high, low, value):
        value = value.reshape(NTH, LANES)
        big = value.astype(jnp.bfloat16)
        small = (value - big.astype(jnp.float32)).astype(jnp.bfloat16)
        out = jnp.dot(high, big, preferred_element_type=jnp.float32)
        out = out + jnp.dot(high, small, preferred_element_type=jnp.float32)
        out = out + jnp.dot(low, big, preferred_element_type=jnp.float32)
        return out.reshape(shape)

    main = product(w_ref[0], w_ref[1], main)
    half = product(w_ref[2], w_ref[3], half)
    packed = jnp.where(lane < 64, half, spread(spread(half, 64, 2), 4, 1))
    for s in range(N_TH):
        base, start = s * BACK_ROWS, s * SEND_ROWS
        out_ref[base : base + 8, :] = main[s]
        out_ref[base + 8 : base + 12, :] = packed[s, :4]
        share_ref[5 * s : 5 * s + 1, :] = r_ref[start + 14 : start + 15, :]
        share_ref[5 * s + 1 : 5 * s + 5, :] = r_ref[start + 16 : start + 20, :]
    share_ref[SHARE:, :] = columns_ref[...]


def filtered(received, matrices, columns):
    return pl.pallas_call(
        filter_kernel,
        in_specs=[WHOLE] * 3,
        out_specs=[WHOLE] * 2,
        out_shape=[
            pltpu.VMEM((N_TH * BACK_ROWS, LANES), jnp.float32),
            pltpu.VMEM((SHARE + NR, LANES), jnp.float32),
        ],
        compiler_params=PARAMS,
        cost_estimate=pl.CostEstimate(flops=6 * 256 * 256 * 256, bytes_accessed=1_200_000, transcendentals=0),
        name="filtered",
    )(in_vmem(received), in_vmem(matrices), in_vmem(columns))


def outer_kernel(odd_ref, d_ref, v_ref, p_ref, side_ref, back_ref, token_ref, out_ref):
    del token_ref
    th_odd = odd_ref[0] == 1
    shape = (NR, LANES)
    lane, row = lanes_of(shape), rows_of(shape)
    radius = row.astype(jnp.float32) + 0.5
    inverse = 1.0 / radius
    c = (theta_factor(0) * 0.5) * inverse

    def load(j):
        return (d_ref[j], v_ref[0, j], v_ref[1, j], v_ref[2, j], p_ref[j])

    def step(j, carry):
        fields = load(j)
        below = load(jnp.maximum(j - 1, 0))
        above = load(jnp.minimum(j + 1, SECTOR - 1))
        use_low, use_high = j == 0, j == SECTOR - 1
        below = [
            jnp.where(use_low, jnp.where(th_odd, side_ref[f], back_ref[f]), below[f]) for f in range(FIELDS)
        ]
        above = [
            jnp.where(use_high, jnp.where(th_odd, back_ref[f], side_ref[f]), above[f]) for f in range(FIELDS)
        ]
        q = conserved(fields)
        radial = flux(fields, q, 0)
        along = flux(fields, q, 2)
        q_low, q_high = conserved(below), conserved(above)
        f_low, f_high = flux(below, q_low, 1), flux(above, q_high, 1)
        scale = 0.25 * inverse
        sources = (
            None,
            scale * (q[2] * fields[2] + fields[4]),
            -scale * (q[1] * fields[2]),
            None,
            None,
        )
        for f in range(FIELDS):
            own = q[f] * (0.8 - 0.8 * c)
            if sources[f] is not None:
                own = own + sources[f]
            smooth, push = SMOOTH * q[f], HALF_STEP * along[f]
            own = own + jnp.where(lane == 0, 0.0, spread(smooth + push, 1, 1))
            own = own + jnp.where(lane == LANES - 1, 0.0, spread(smooth - push, LANES - 1, 1))
            own = own + c * (0.4 * (q_low[f] + q_high[f]) + (f_low[f] - f_high[f]))
            push = (HALF_STEP * radius) * radial[f]
            smooth_ahead = jnp.where(row == NR - 1, smooth, spread(smooth, NR - 1, 0))
            push_ahead = jnp.where(row == NR - 1, push + HALF_STEP * radial[f], spread(push, NR - 1, 0))
            own = own + (smooth_ahead + spread(smooth, 1, 0))
            own = own + inverse * (spread(push, 1, 0) - push_ahead)
            out_ref[f, j] = own
        return carry

    lax.fori_loop(0, SECTOR, step, 0)


def outer_part(odd, density, velocity, pressure, side, back, token):
    return pl.pallas_call(
        outer_kernel,
        in_specs=[SCALARS] + [WHOLE] * 5 + [pl.BlockSpec(memory_space=pl.ANY)],
        out_specs=WHOLE,
        out_shape=pltpu.VMEM((FIELDS, SECTOR, NR, LANES), jnp.float32),
        compiler_params=PARAMS,
        cost_estimate=pl.CostEstimate(flops=64 * 1024 * 250, bytes_accessed=3_000_000, transcendentals=0),
        name="outer_part",
    )(odd, density, velocity, pressure, in_vmem(side), in_vmem(back), token)


def finish_kernel(place_ref, r_ref, w_ref, near_ref, far_ref, rest_ref, out_ref, buffer, border, done):
    start = N_TH - 1 - place_ref[0]
    odd = place_ref[1] == 1
    near, far = near_ref[...], far_ref[...]
    before, after = jnp.where(odd, near, far), jnp.where(odd, far, near)
    border[...] = jnp.where(lanes_of((SHARE, LANES)) % 2 == 1, before[:SHARE], after[:SHARE])
    terms = axial_terms(before[SHARE + NF :], after[SHARE + NF :])
    shape = (SECTOR, LANES)
    lane = lanes_of(shape)
    ends = (lane == 0) | (lane == LANES - 1)
    low_half = lanes_of((4, LANES)) < 64
    far_lane = lanes_of((NR - NF, LANES))
    far_ends = (far_lane == 0) | (far_lane == LANES - 1)

    def outer(j):
        rows = pl.ds(NF, NR - NF)
        return pltpu.make_async_copy(buffer.at[:, j, rows, :], out_ref.at[:, j, rows, :], done.at[j])

    for j in range(SECTOR):
        for f in range(FIELDS):
            side = spread(terms[f], LANES - 1 - 2 * j, 1)
            buffer[f, j, NF:, :] = rest_ref[f, j, NF:, :] + jnp.where(far_ends, side, 0.0)
        outer(j).start()

    sums = [jnp.zeros(shape, jnp.float32) for _ in range(FIELDS)]
    for t in range(N_TH):
        weights = w_ref[start + t]
        for f in range(FIELDS):
            sums[f] = sums[f] + weights * border[5 * t + f : 5 * t + f + 1, :]
    for f in range(FIELDS):
        for shift in (2, 4, 8):
            sums[f] = sums[f] + spread(sums[f], -shift, 1)

    def joined(unit_a, unit_b):
        a = r_ref[unit_a * BACK_ROWS + 8 : unit_a * BACK_ROWS + 12, :]
        b = r_ref[unit_b * BACK_ROWS + 8 : unit_b * BACK_ROWS + 12, :]
        top = jnp.where(low_half, a, spread(b, 64, 1))
        bottom = jnp.where(low_half, spread(a, 64, 1), b)
        return jnp.concatenate([top, bottom], axis=0)

    for f in range(FIELDS):
        for cycle in range(NF):
            if f < 4:
                unit = (f * NF + cycle) * BACK_ROWS
                tile = r_ref[unit : unit + 8, :]
            else:
                tile = joined(cycle, NF + cycle)
            if cycle == 0:
                tile = tile + joined(16 + 2 * f, 17 + 2 * f)
            tile = tile + jnp.where(ends, spread(sums[f], -(16 * cycle + 1), 1), 0.0)
            buffer[f, :, cycle, :] = tile
    rows = pl.ds(0, NF)
    inner = pltpu.make_async_copy(buffer.at[:, :, rows, :], out_ref.at[:, :, rows, :], done.at[SECTOR])
    inner.start()
    for j in range(SECTOR):
        outer(j).wait()
    inner.wait()


def finish(place, received, weights, near, far, rest):
    block = (FIELDS, SECTOR, NR, LANES)
    return pl.pallas_call(
        finish_kernel,
        in_specs=[SCALARS] + [WHOLE] * 5,
        out_specs=pl.BlockSpec(memory_space=pl.ANY),
        out_shape=jax.ShapeDtypeStruct(block, jnp.float32),
        scratch_shapes=[
            pltpu.VMEM(block, jnp.float32),
            pltpu.VMEM((SHARE, LANES), jnp.float32),
            pltpu.SemaphoreType.DMA((SECTOR + 1,)),
        ],
        compiler_params=PARAMS,
        cost_estimate=pl.CostEstimate(flops=400 * 1024, bytes_accessed=3_000_000, transcendentals=0),
        name="finish",
    )(place, in_vmem(received), in_vmem(weights), in_vmem(near), in_vmem(far), in_vmem(rest))


def pairs(size, offset):
    return [(i, (((i - offset) ^ 1) + offset) % size) for i in range(size)]


def transposed(value, rows):
    value = value.reshape(N_TH, rows // 4, 4, LANES)
    return lax.all_to_all(value, "th", 0, 0, tiled=True).reshape(N_TH * rows, LANES)


def per_device(density, velocity, pressure):
    high, low = filter_matrices()
    high, low = jnp.asarray(high), jnp.asarray(low)
    weights = jnp.asarray(edge_weights())
    th, gz = lax.axis_index("th"), lax.axis_index("gz")
    main = th % NF
    half = jnp.where(th < 16, main, jnp.where(th < 26, NF, 0))
    which = jnp.stack([th % 2, main, half]).astype(jnp.int32)
    place = jnp.stack([th, gz % 2]).astype(jnp.int32)

    sent = inner_part(density, velocity, pressure)
    received = transposed(sent, SEND_ROWS)

    near_row, far_row, columns, matrices = edges(which, high, low, density, velocity, pressure)
    th_far = lax.ppermute(far_row, "th", pairs(N_TH, 1))
    th_near = lax.ppermute(near_row, "th", pairs(N_TH, 0))

    back, share = filtered(received, matrices, columns)
    back, th_far, th_near = lax.optimization_barrier((back, th_far, th_near))
    returned = transposed(back, BACK_ROWS)
    gz_size = lax.axis_size("gz")
    gz_far = lax.ppermute(share, "gz", pairs(gz_size, 1))
    gz_near = lax.ppermute(share, "gz", pairs(gz_size, 0))
    rest = outer_part(which, density, velocity, pressure, th_near, th_far, share)
    return finish(place, returned, weights, gz_near, gz_far, rest)


def solution(mesh):
    in_specs = (P("th", None, "gz"), P(None, "th", None, "gz"), P("th", None, "gz"))
    out_specs = P(None, "th", None, "gz")
    return jax.shard_map(
        per_device, mesh=mesh, in_specs=in_specs, out_specs=out_specs, check_vma=False
    )
```

```python
import math

import jax
import jax.numpy as jnp
import ml_dtypes
import numpy as np
from jax import lax
from jax.experimental import pallas as pl
from jax.experimental.pallas import tpu as pltpu
from jax.sharding import PartitionSpec as P

NTH = 256
NR = 64
NF = 8
N_TH = 32
SECTOR = NTH // N_TH
LANES = 128
FIELDS = 5
SEND_ROWS = 20
BACK_ROWS = 12
SHARE = N_TH * FIELDS
HALF_SHARE = SHARE // 2
OUTER = NR - NF
BLOCK_ROWS = FIELDS * SECTOR * OUTER
PARITY_ROW = BLOCK_ROWS + N_TH * SECTOR
REST_ROWS = PARITY_ROW + SECTOR
FIRST = 24
ROW_FIELDS = 10

HALF_STEP = 0.125
SMOOTH = 0.05


def theta_factor(cycle):
    return 0.25 / (2.0 * (2.0 * math.pi / NTH) * (cycle + 0.5))


def filter_rows():
    modes = np.arange(NTH)
    folded = np.minimum(modes, NTH - modes)
    waves = np.cos(2.0 * math.pi * (modes[:, None] * modes[None, :] % NTH) / NTH)
    rows = []
    for cycle in range(NF):
        keep = 2 * (NF + 1) * folded <= NTH * (cycle + 1)
        rows.append(waves[:, keep].sum(axis=1) / NTH)
    return np.stack(rows)


def filter_matrices():
    rows = filter_rows()
    index = (np.arange(NTH)[:, None] - np.arange(NTH)[None, :]) % NTH
    full = np.concatenate([rows[:, index], rows[:1, (index + NTH // 2) % NTH]]).astype(np.float32)
    high = full.astype(ml_dtypes.bfloat16)
    low = (full - high.astype(np.float32)).astype(ml_dtypes.bfloat16)
    return high, low


def edge_weights():
    rows = filter_rows()
    table = np.zeros((2 * N_TH, SECTOR, LANES), np.float32)
    for row in range(2 * N_TH - 1):
        apart = (N_TH - 1 - row) * SECTOR
        index = (apart + np.arange(SECTOR)[:, None] - np.arange(SECTOR)[None, :]) % NTH
        block = np.repeat(rows[:, index].transpose(1, 0, 2)[..., None], 2, axis=3)
        table[row] = block.reshape(SECTOR, LANES)
    return table.reshape(2 * N_TH * SECTOR, LANES)


def conserved(fields):
    rho, ur, ut, uz, p = fields
    qr, qt, qz = rho * ur, rho * ut, rho * uz
    energy = p * 2.5 + 0.5 * (qr * ur + qt * ut + qz * uz)
    return rho, qr, qt, qz, energy


def flux(fields, q, direction):
    p = fields[4]
    speed = fields[1 + direction]
    moving = q[1 + direction]
    parts = [moving, moving * fields[1], moving * fields[2], moving * fields[3], speed * (q[4] + p)]
    parts[1 + direction] = parts[1 + direction] + p
    return parts


def slot(sector):
    return (sector - FIRST) % N_TH


def lanes_of(shape):
    return lax.broadcasted_iota(jnp.int32, shape, len(shape) - 1)


def rows_of(shape):
    return lax.broadcasted_iota(jnp.int32, shape, len(shape) - 2)


def spread(value, shift, axis):
    size = value.shape[axis]
    return pltpu.roll(value, shift % size, axis)


def half_packs(tile):
    turned = spread(tile, 64, 1)
    low = lanes_of((SECTOR, LANES)) < 64
    first = jnp.where(low, tile, spread(turned, 4, 0))
    second = jnp.where(low, turned, spread(tile, 4, 0))
    return first[:4], second[:4]


def inner_kernel(d_ref, v_ref, p_ref, out_ref):
    size = 16 * SECTOR
    d_rows, v_rows, p_rows = (
        d_ref.reshape(size, LANES), v_ref.reshape(3 * size, LANES), p_ref.reshape(size, LANES)
    )

    def load(cycle):
        def rows(ref, first):
            return ref[pl.ds(first + cycle, SECTOR, stride=16), :]

        return (rows(d_rows, 0), *[rows(v_rows, n * size) for n in range(3)], rows(p_rows, 0))

    def store(unit, row, value):
        start = slot(unit) * SEND_ROWS + row
        out_ref[start : start + value.shape[0], :] = value

    shape = (SECTOR, LANES)
    lane, row = lanes_of(shape), rows_of(shape)
    first_lane, last_lane = lane == 0, lane == LANES - 1
    not_first_row, not_last_row = row > 0, row < SECTOR - 1
    low = lanes_of((1, LANES)) < 64
    for unit in range(16, N_TH):
        store(unit, 9, jnp.zeros((5, LANES), jnp.float32))

    before = None
    fields = load(0)
    q = conserved(fields)
    radial = flux(fields, q, 0)
    for f in range(FIELDS):
        sign = -1.0 if f in (1, 2) else 1.0
        mirrored = sign * (SMOOTH * q[f] + HALF_STEP * radial[f])
        for half, pack in enumerate(half_packs(mirrored)):
            store(16 + 2 * f + half, 10, pack)
    border = [jnp.zeros(shape, jnp.float32) for _ in range(FIELDS)]
    for cycle in range(NF):
        after_fields = load(cycle + 1)
        after_q = conserved(after_fields)
        after = (after_q, flux(after_fields, after_q, 0))
        around = flux(fields, q, 1)
        along = flux(fields, q, 2)
        c = theta_factor(cycle)
        radius = cycle + 0.5
        scale = 0.25 / radius
        sources = (
            None,
            scale * (q[2] * fields[2] + fields[4]),
            -scale * (q[1] * fields[2]),
            None,
            None,
        )
        for f in range(FIELDS):
            own = q[f] * (0.8 - 0.8 * c)
            if sources[f] is not None:
                own = own + sources[f]
            smooth, push = SMOOTH * q[f], HALF_STEP * along[f]
            forward, backward = spread(smooth + push, 1, 1), spread(smooth - push, -1, 1)
            own = own + jnp.where(first_lane, 0.0, forward) + jnp.where(last_lane, 0.0, backward)
            beyond = jnp.where(first_lane, forward, jnp.where(last_lane, backward, 0.0))
            border[f] = border[f] + spread(beyond, 16 * cycle + 1, 1)
            smooth, push = (0.4 * c) * q[f], c * around[f]
            rising, falling = smooth + push, smooth - push
            own = own + jnp.where(not_first_row, spread(rising, 1, 0), 0.0)
            own = own + jnp.where(not_last_row, spread(falling, -1, 0), 0.0)
            own = own + (SMOOTH * after[0][f] - (HALF_STEP * (radius + 1.0) / radius) * after[1][f])
            if before is not None:
                own = own + (SMOOTH * before[0][f] + (HALF_STEP * (radius - 1.0) / radius) * before[1][f])
            up, down = rising[7:8], falling[0:1]
            if f < 4:
                unit = f * NF + cycle
                store(unit, 0, own)
                store(unit, 8, up)
                store(unit, 15, down)
            else:
                packs = half_packs(own)
                store(cycle, 10, packs[0])
                store(cycle, 9, jnp.where(low, down, spread(up, 64, 1)))
                store(NF + cycle, 10, packs[1])
                store(NF + cycle, 9, jnp.where(low, spread(down, 64, 1), up))
        before = (q, radial)
        fields, q, radial = after_fields, after_q, after[1]
    rows = [
        jnp.sum(pltpu.roll(value, 0, 1, stride=2, stride_axis=0), axis=0, keepdims=True) for value in border
    ]
    others = jnp.concatenate(rows[1:], axis=0)
    for unit in range(N_TH):
        store(unit, 14, rows[0])
        store(unit, 16, others)


def in_vmem(value):
    return pltpu.with_memory_space_constraint(value, pltpu.VMEM)


def in_hbm(value):
    return pltpu.with_memory_space_constraint(value, pltpu.HBM)


PARAMS = pltpu.CompilerParams(vmem_limit_bytes=24 << 20)
WHOLE = pl.BlockSpec(memory_space=pltpu.VMEM)
SCALARS = pl.BlockSpec(memory_space=pltpu.SMEM)


def inner_part(density, velocity, pressure):
    return pl.pallas_call(
        inner_kernel,
        grid=(1,),
        in_specs=[
            pl.BlockSpec((SECTOR, 16, LANES), lambda i: (0, 0, 0)),
            pl.BlockSpec((3, SECTOR, 16, LANES), lambda i: (0, 0, 0, 0)),
            pl.BlockSpec((SECTOR, 16, LANES), lambda i: (0, 0, 0)),
        ],
        out_specs=WHOLE,
        out_shape=pltpu.VMEM((N_TH * SEND_ROWS, LANES), jnp.float32),
        compiler_params=PARAMS,
        cost_estimate=pl.CostEstimate(flops=8 * 1024 * 200, bytes_accessed=600_000, transcendentals=0),
        name="inner_part",
    )(in_hbm(density), in_hbm(velocity), in_hbm(pressure))


def edge_kernel(which_ref, d_ref, v_ref, p_ref, near_ref, far_ref, columns_ref):
    lane = lanes_of((NR, LANES))
    odd = which_ref[0] == 1

    def load(f, j):
        return d_ref[j] if f == 0 else (p_ref[j] if f == 4 else v_ref[f - 1, j])

    firsts = jnp.zeros((NR, LANES), jnp.float32)
    lasts = firsts
    for f in range(FIELDS):
        for j in range(SECTOR):
            spot = 16 * f + 2 * j
            value = spread(load(f, j), spot + 1, 1)
            firsts = jnp.where(lane == spot + 1, value, firsts)
            lasts = jnp.where(lane == spot, value, lasts)
        first, last = load(f, 0), load(f, SECTOR - 1)
        near_ref[f] = jnp.where(odd, first, last)
        far_ref[f] = jnp.where(odd, last, first)
    columns_ref[...] = spread(firsts, -1, 1) + spread(lasts, 1, 1)


def edges(which, density, velocity, pressure):
    rows = pltpu.VMEM((ROW_FIELDS, NR, LANES), jnp.float32)
    return pl.pallas_call(
        edge_kernel,
        in_specs=[SCALARS] + [WHOLE] * 3,
        out_specs=[WHOLE] * 3,
        out_shape=[rows, rows, pltpu.VMEM((NR, LANES), jnp.float32)],
        compiler_params=PARAMS,
        cost_estimate=pl.CostEstimate(flops=320 * 1024 * 3, bytes_accessed=1_800_000, transcendentals=0),
        name="edges",
    )(which, in_vmem(density), in_vmem(velocity), in_vmem(pressure))


def axial_terms(both):
    lane = lanes_of(both.shape)
    fields = [both] + [spread(both, -16 * f, 1) for f in range(1, FIELDS)]
    q = conserved(fields)
    along = flux(fields, q, 2)
    push = jnp.where(lane % 2 == 1, HALF_STEP, -HALF_STEP)
    return [SMOOTH * q[f] + push * along[f] for f in range(FIELDS)]


def filter_kernel(r_ref, w_ref, columns_ref, out_ref, next_ref, last_ref, share):
    shape = (N_TH, SECTOR, LANES)
    row, lane = rows_of(shape), lanes_of(shape)
    starts = [slot(s) * SEND_ROWS for s in range(N_TH)]
    main = jnp.stack([r_ref[a : a + 8, :] for a in starts])
    extra = jnp.stack([r_ref[a + 8 : a + 16, :] for a in starts])
    zero = jnp.zeros(shape, jnp.float32)

    def earlier(value):
        return jnp.concatenate([value[-1:], value[:-1]], axis=0)

    def later(value):
        return jnp.concatenate([value[1:], value[:1]], axis=0)

    main = main + jnp.where(row == 0, earlier(extra), jnp.where(row == 7, later(extra), zero))
    turned = spread(extra, 64, 2)
    top = spread(extra, 6, 1)
    half = jnp.where(row < 4, top, spread(turned, 2, 1))
    half = half + jnp.where(
        row == 0, earlier(spread(turned, 7, 1)), jnp.where(row == 7, later(top), zero)
    )

    def product(high, low, value):
        value = value.reshape(NTH, LANES)
        big = value.astype(jnp.bfloat16)
        small = (value - big.astype(jnp.float32)).astype(jnp.bfloat16)
        out = jnp.dot(high, big, preferred_element_type=jnp.float32)
        out = out + jnp.dot(high, small, preferred_element_type=jnp.float32)
        out = out + jnp.dot(low, big, preferred_element_type=jnp.float32)
        return out.reshape(shape)

    main = product(w_ref[0], w_ref[1], main)
    half = product(w_ref[2], w_ref[3], half)
    packed = jnp.where(lane < 64, half, spread(spread(half, 64, 2), 4, 1))
    for s in range(N_TH):
        base, start = slot(s) * BACK_ROWS, starts[s]
        out_ref[base : base + 8, :] = main[s]
        out_ref[base + 8 : base + 12, :] = packed[s, :4]
        share[5 * s : 5 * s + 1, :] = r_ref[start + 14 : start + 15, :]
        share[5 * s + 1 : 5 * s + 5, :] = r_ref[start + 16 : start + 20, :]
    values = share[...]
    columns = columns_ref[...]
    for place, upper, lower in (
        (slice(0, HALF_SHARE), values[:HALF_SHARE], values[HALF_SHARE:]),
        (slice(HALF_SHARE, None), columns[: NR // 2], columns[NR // 2 :]),
    ):
        next_ref[place, :], last_ref[place, :] = two_halves(upper, lower)


def two_halves(upper, lower):
    odd = lanes_of(upper.shape) % 2 == 1
    return jnp.where(odd, upper, spread(lower, -1, 1)), jnp.where(odd, spread(upper, 1, 1), lower)


def from_halves(odd_lanes, even_lanes):
    odd = lanes_of(odd_lanes.shape) % 2 == 1
    upper = jnp.where(odd, odd_lanes, spread(even_lanes, -1, 1))
    lower = jnp.where(odd, spread(odd_lanes, 1, 1), even_lanes)
    return upper, lower


def filtered(received, matrices, columns):
    pack = pltpu.VMEM((HALF_SHARE + NR // 2, LANES), jnp.float32)
    return pl.pallas_call(
        filter_kernel,
        in_specs=[WHOLE] * 3,
        out_specs=[WHOLE] * 3,
        out_shape=[pltpu.VMEM((N_TH * BACK_ROWS, LANES), jnp.float32), pack, pack],
        scratch_shapes=[pltpu.VMEM((SHARE, LANES), jnp.float32)],
        compiler_params=PARAMS,
        cost_estimate=pl.CostEstimate(flops=6 * 256 * 256 * 256, bytes_accessed=1_200_000, transcendentals=0),
        name="filtered",
    )(in_vmem(received), in_vmem(matrices), in_vmem(columns))


def theta_terms(fields, q, c):
    around = flux(fields, q, 1)
    smooth = [(0.4 * c) * part for part in q]
    push = [c * part for part in around]
    return [a + b for a, b in zip(smooth, push)], [a - b for a, b in zip(smooth, push)]


def outer_kernel(
    which_ref, high_ref, low_ref, table_ref, d_ref, v_ref, p_ref, out_ref, w_ref, rising_ref, done
):
    copies = [
        pltpu.make_async_copy(table.at[which_ref[1 + k]], w_ref.at[2 * k + n], done.at[2 * k + n])
        for k in range(2)
        for n, table in enumerate((high_ref, low_ref))
    ]
    first = pl.multiple_of(which_ref[3] * SECTOR, SECTOR)
    size = N_TH * SECTOR
    copies.append(
        pltpu.make_async_copy(
            table_ref.at[pl.ds(first, size), :], out_ref.at[pl.ds(BLOCK_ROWS, size), :], done.at[4]
        )
    )
    for copy in copies:
        copy.start()
    out_ref[PARITY_ROW:, :] = jnp.full((SECTOR, LANES), which_ref[0].astype(jnp.float32))
    shape = (NR, LANES)
    lane, row = lanes_of(shape)[NF:], rows_of(shape)
    radius = row.astype(jnp.float32) + 0.5
    inverse = (1.0 / radius)[NF:]
    c = (theta_factor(0) * 0.5) * inverse
    first_lane, last_lane = lane == 0, lane == LANES - 1
    last_row = row == NR - 1
    own_scale, source_scale = 0.8 - 0.8 * c, 0.25 * inverse
    push_scale = HALF_STEP * radius
    for f in range(FIELDS):
        rising_ref[f] = jnp.zeros((NR - NF, LANES), jnp.float32)

    def rows_at(f, j):
        return pl.ds(pl.multiple_of((f * SECTOR + j) * OUTER, NF), OUTER)

    def step(j, carry):
        every = (d_ref[j], v_ref[0, j], v_ref[1, j], v_ref[2, j], p_ref[j])
        every_q = conserved(every)
        radial = flux(every, every_q, 0)
        fields, q = [part[NF:] for part in every], [part[NF:] for part in every_q]
        along = flux(fields, q, 2)
        rising, falling = theta_terms(fields, q, c)
        sources = (
            None,
            source_scale * (q[2] * fields[2] + fields[4]),
            -source_scale * (q[1] * fields[2]),
            None,
            None,
        )
        for f in range(FIELDS):
            own = q[f] * own_scale
            if sources[f] is not None:
                own = own + sources[f]
            smooth, push = SMOOTH * every_q[f], HALF_STEP * along[f]
            near = smooth[NF:]
            own = own + jnp.where(first_lane, 0.0, spread(near + push, 1, 1))
            own = own + jnp.where(last_lane, 0.0, spread(near - push, LANES - 1, 1))
            push = push_scale * radial[f]
            ghost = push + HALF_STEP * radial[f]
            smooth_ahead = jnp.where(last_row, smooth, spread(smooth, NR - 1, 0))
            push_ahead = jnp.where(last_row, ghost, spread(push, NR - 1, 0))
            own = own + (smooth_ahead + spread(smooth, 1, 0))[NF:]
            own = own + inverse * (spread(push, 1, 0) - push_ahead)[NF:]
            out_ref[rows_at(f, j), :] = own + rising_ref[f]
            rising_ref[f] = rising[f]

        @pl.when(j > 0)
        def _():
            for f in range(FIELDS):
                out_ref[rows_at(f, j - 1), :] = out_ref[rows_at(f, j - 1), :] + falling[f]

        return carry

    lax.fori_loop(0, SECTOR, step, 0)
    for copy in copies:
        copy.wait()


def outer_part(which, high, low, table, density, velocity, pressure):
    return pl.pallas_call(
        outer_kernel,
        in_specs=[SCALARS] + [pl.BlockSpec(memory_space=pl.ANY)] * 3 + [WHOLE] * 3,
        out_specs=[WHOLE] * 2,
        out_shape=[
            pltpu.VMEM((REST_ROWS, LANES), jnp.float32),
            pltpu.VMEM((4, NTH, NTH), jnp.bfloat16),
        ],
        scratch_shapes=[
            pltpu.VMEM((FIELDS, NR - NF, LANES), jnp.float32),
            pltpu.SemaphoreType.DMA((5,)),
        ],
        compiler_params=PARAMS,
        cost_estimate=pl.CostEstimate(flops=64 * 1024 * 250, bytes_accessed=3_000_000, transcendentals=0),
        name="outer_part",
    )(
        which,
        *[in_hbm(value) for value in (high, low, table)],
        *[in_vmem(value) for value in (density, velocity, pressure)],
    )


def finish_kernel(
    r_ref, before_ref, after_ref, rest_ref, side_ref, back_ref, out_ref, buffer, border, rows_ref, done
):
    arrivals = [
        pltpu.make_async_copy(
            value.at[pl.ds(0, FIELDS), pl.ds(NF, NR - NF), :], rows_ref.at[n], done.at[SECTOR + 1 + n]
        )
        for n, value in enumerate((side_ref, back_ref))
    ]
    for copy in arrivals:
        copy.start()
    before, after = before_ref[...], after_ref[...]
    upper, lower = from_halves(before, after)
    border[:HALF_SHARE, :] = upper[:HALF_SHARE]
    border[HALF_SHARE:, :] = lower[:HALF_SHARE]
    terms = axial_terms(jnp.concatenate([upper[HALF_SHARE:], lower[HALF_SHARE:]], axis=0)[NF:])
    shape = (SECTOR, LANES)
    lane = lanes_of(shape)
    ends = (lane == 0) | (lane == LANES - 1)
    low_half = lanes_of((4, LANES)) < 64
    far_lane = lanes_of((NR - NF, LANES))
    far_ends = (far_lane == 0) | (far_lane == LANES - 1)

    def outer(j):
        rows = pl.ds(NF, NR - NF)
        return pltpu.make_async_copy(buffer.at[:, j, rows, :], out_ref.at[:, j, rows, :], done.at[j])

    def write_outer(j, more):
        for f in range(FIELDS):
            beyond = jnp.where(far_ends, spread(terms[f], LANES - 1 - 2 * j, 1), 0.0)
            if more is not None:
                beyond = beyond + more[f]
            first = (f * SECTOR + j) * OUTER
            buffer[f, j, NF:, :] = rest_ref[first : first + OUTER, :] + beyond
        outer(j).start()

    for j in range(1, SECTOR - 1):
        write_outer(j, None)

    sums = [jnp.zeros(shape, jnp.float32) for _ in range(FIELDS)]
    for t in range(N_TH):
        weights = rest_ref[BLOCK_ROWS + SECTOR * t : BLOCK_ROWS + SECTOR * (t + 1), :]
        for f in range(FIELDS):
            sums[f] = sums[f] + weights * border[5 * t + f : 5 * t + f + 1, :]
    for f in range(FIELDS):
        for shift in (2, 4, 8):
            sums[f] = sums[f] + spread(sums[f], -shift, 1)

    tiles = buffer.reshape(FIELDS * SECTOR * NR, LANES)

    def joined(unit_a, unit_b):
        start_a, start_b = slot(unit_a) * BACK_ROWS + 8, slot(unit_b) * BACK_ROWS + 8
        a, b = r_ref[start_a : start_a + 4, :], r_ref[start_b : start_b + 4, :]
        top = jnp.where(low_half, a, spread(b, 64, 1))
        bottom = jnp.where(low_half, spread(a, 64, 1), b)
        return jnp.concatenate([top, bottom], axis=0)

    for f in range(FIELDS):
        for cycle in range(NF):
            if f < 4:
                start = slot(f * NF + cycle) * BACK_ROWS
                tile = r_ref[start : start + 8, :]
            else:
                tile = joined(cycle, NF + cycle)
            if cycle == 0:
                tile = tile + joined(16 + 2 * f, 17 + 2 * f)
            tile = tile + jnp.where(ends, spread(sums[f], -(16 * cycle + 1), 1), 0.0)
            tiles[pl.ds(f * SECTOR * NR + cycle, SECTOR, stride=NR), :] = tile
    rows = pl.ds(0, NF)
    inner = pltpu.make_async_copy(buffer.at[:, :, rows, :], out_ref.at[:, :, rows, :], done.at[SECTOR])
    inner.start()
    for copy in arrivals:
        copy.wait()
    c = (theta_factor(0) * 0.5) / (rows_of((NR, LANES))[NF:].astype(jnp.float32) + 0.5)
    odd = jnp.concatenate([rest_ref[PARITY_ROW:, :]] * (NR // NF - 1), axis=0) > 0.5
    side = [rows_ref[0, f] for f in range(FIELDS)]
    back = [rows_ref[1, f] for f in range(FIELDS)]
    below = [jnp.where(odd, a, b) for a, b in zip(side, back)]
    above = [jnp.where(odd, b, a) for a, b in zip(side, back)]
    write_outer(0, theta_terms(below, conserved(below), c)[0])
    write_outer(SECTOR - 1, theta_terms(above, conserved(above), c)[1])
    for j in range(SECTOR):
        outer(j).wait()
    inner.wait()


def finish(received, before, after, rest, side, back):
    block = (FIELDS, SECTOR, NR, LANES)
    return pl.pallas_call(
        finish_kernel,
        in_specs=[WHOLE] * 4 + [pl.BlockSpec(memory_space=pl.ANY)] * 2,
        out_specs=pl.BlockSpec(memory_space=pl.ANY),
        out_shape=jax.ShapeDtypeStruct(block, jnp.float32),
        scratch_shapes=[
            pltpu.VMEM(block, jnp.float32),
            pltpu.VMEM((SHARE, LANES), jnp.float32),
            pltpu.VMEM((2, FIELDS, NR - NF, LANES), jnp.float32),
            pltpu.SemaphoreType.DMA((SECTOR + 3,)),
        ],
        compiler_params=PARAMS,
        cost_estimate=pl.CostEstimate(flops=400 * 1024, bytes_accessed=3_000_000, transcendentals=0),
        name="finish",
    )(
        *[in_vmem(value) for value in (received, before, after, rest)],
        in_hbm(side),
        in_hbm(back),
    )


def pairs(size, offset):
    return [(i, (((i - offset) ^ 1) + offset) % size) for i in range(size)]


def transposed(value, rows):
    value = value.reshape(N_TH, rows // 4, 4, LANES)
    group = [(FIRST + k) % N_TH for k in range(N_TH)]
    value = lax.all_to_all(value, "th", 0, 0, tiled=True, axis_index_groups=[group])
    return value.reshape(N_TH * rows, LANES)


def per_device(density, velocity, pressure):
    high, low = filter_matrices()
    high, low = jnp.asarray(high), jnp.asarray(low)
    table = jnp.asarray(edge_weights())
    th = lax.axis_index("th")
    main = th % NF
    half = jnp.where(th < 16, main, jnp.where(th < 26, NF, 0))
    which = jnp.stack([th % 2, main, half, N_TH - 1 - th]).astype(jnp.int32)

    sent = inner_part(density, velocity, pressure)
    received = transposed(sent, SEND_ROWS)

    near_row, far_row, columns = edges(which, density, velocity, pressure)
    th_far = lax.ppermute(far_row, "th", pairs(N_TH, 1))
    th_near = lax.ppermute(near_row, "th", pairs(N_TH, 0))

    rest, matrices = outer_part(which, high, low, table, density, velocity, pressure)
    back, to_next, to_last = filtered(received, matrices, columns)
    to_next, to_last, th_far, th_near = lax.optimization_barrier((to_next, to_last, th_far, th_near))
    returned = transposed(back, BACK_ROWS)
    size = lax.axis_size("gz")
    before = lax.ppermute(to_next, "gz", [(i, (i + 1) % size) for i in range(size)])
    after = lax.ppermute(to_last, "gz", [(i, (i - 1) % size) for i in range(size)])
    return finish(returned, before, after, rest, th_near, th_far)


def solution(mesh):
    in_specs = (P("th", None, "gz"), P(None, "th", None, "gz"), P("th", None, "gz"))
    out_specs = P(None, "th", None, "gz")
    return jax.shard_map(
        per_device, mesh=mesh, in_specs=in_specs, out_specs=out_specs, check_vma=False
    )
```

```python
import math

import jax
import jax.numpy as jnp
import ml_dtypes
import numpy as np
from jax import lax
from jax.experimental import pallas as pl
from jax.experimental.pallas import tpu as pltpu
from jax.sharding import PartitionSpec as P

NTH = 256
NR = 64
NF = 8
N_TH = 32
SECTOR = NTH // N_TH
LANES = 128
FIELDS = 5
SEND_ROWS = 20
BACK_ROWS = 12
OUTER = NR - NF
BLOCK_ROWS = FIELDS * SECTOR * OUTER
PACK_ROWS = SECTOR + NR // 2
UP_ROWS, DOWN_ROWS = 0, 0
FIRST = 24
ROW_FIELDS = 11

HALF_STEP = 0.125
SMOOTH = 0.05


def theta_factor(cycle):
    return 0.25 / (2.0 * (2.0 * math.pi / NTH) * (cycle + 0.5))


def filter_rows():
    modes = np.arange(NTH)
    folded = np.minimum(modes, NTH - modes)
    waves = np.cos(2.0 * math.pi * (modes[:, None] * modes[None, :] % NTH) / NTH)
    rows = []
    for cycle in range(NF):
        keep = 2 * (NF + 1) * folded <= NTH * (cycle + 1)
        rows.append(waves[:, keep].sum(axis=1) / NTH)
    return np.stack(rows)


def filter_matrices():
    rows = filter_rows()
    index = (np.arange(NTH)[:, None] - np.arange(NTH)[None, :]) % NTH
    full = np.concatenate([rows[:, index], rows[:1, (index + NTH // 2) % NTH]]).astype(np.float32)
    high = full.astype(ml_dtypes.bfloat16)
    low = (full - high.astype(np.float32)).astype(ml_dtypes.bfloat16)
    return high, low


def edge_weights():
    rows = filter_rows()
    table = np.zeros((2 * N_TH, SECTOR, LANES), np.float32)
    for row in range(2 * N_TH - 1):
        apart = (N_TH - 1 - row) * SECTOR
        index = (apart + np.arange(SECTOR)[:, None] - np.arange(SECTOR)[None, :]) % NTH
        block = np.repeat(rows[:, index].transpose(1, 0, 2)[..., None], 2, axis=3)
        table[row] = block.reshape(SECTOR, LANES)
    return table.reshape(2 * N_TH * SECTOR, LANES)


def conserved(fields):
    rho, ur, ut, uz, p = fields
    qr, qt, qz = rho * ur, rho * ut, rho * uz
    energy = p * 2.5 + 0.5 * (qr * ur + qt * ut + qz * uz)
    return rho, qr, qt, qz, energy


def flux(fields, q, direction):
    p = fields[4]
    speed = fields[1 + direction]
    moving = q[1 + direction]
    parts = [moving, moving * fields[1], moving * fields[2], moving * fields[3], speed * (q[4] + p)]
    parts[1 + direction] = parts[1 + direction] + p
    return parts


def slot(sector):
    return (sector - FIRST) % N_TH


def lanes_of(shape):
    return lax.broadcasted_iota(jnp.int32, shape, len(shape) - 1)


def rows_of(shape):
    return lax.broadcasted_iota(jnp.int32, shape, len(shape) - 2)


def spread(value, shift, axis):
    size = value.shape[axis]
    return pltpu.roll(value, shift % size, axis)


def half_packs(tile):
    turned = spread(tile, 64, 1)
    low = lanes_of((SECTOR, LANES)) < 64
    first = jnp.where(low, tile, spread(turned, 4, 0))
    second = jnp.where(low, turned, spread(tile, 4, 0))
    return first[:4], second[:4]


def inner_kernel(d_ref, v_ref, p_ref, out_ref):
    size = 16 * SECTOR
    d_rows, v_rows, p_rows = (
        d_ref.reshape(size, LANES), v_ref.reshape(3 * size, LANES), p_ref.reshape(size, LANES)
    )

    def load(cycle):
        def rows(ref, first):
            return ref[pl.ds(first + cycle, SECTOR, stride=16), :]

        return (rows(d_rows, 0), *[rows(v_rows, n * size) for n in range(3)], rows(p_rows, 0))

    def store(unit, row, value):
        start = slot(unit) * SEND_ROWS + row
        out_ref[start : start + value.shape[0], :] = value

    shape = (SECTOR, LANES)
    lane, row = lanes_of(shape), rows_of(shape)
    first_lane, last_lane = lane == 0, lane == LANES - 1
    not_first_row, not_last_row = row > 0, row < SECTOR - 1
    low = lanes_of((1, LANES)) < 64
    for unit in range(16, N_TH):
        store(unit, 9, jnp.zeros((5, LANES), jnp.float32))

    before = None
    fields = load(0)
    q = conserved(fields)
    radial = flux(fields, q, 0)
    for f in range(FIELDS):
        sign = -1.0 if f in (1, 2) else 1.0
        mirrored = sign * (SMOOTH * q[f] + HALF_STEP * radial[f])
        for half, pack in enumerate(half_packs(mirrored)):
            store(16 + 2 * f + half, 10, pack)
    border = [jnp.zeros(shape, jnp.float32) for _ in range(FIELDS)]
    for cycle in range(NF):
        after_fields = load(cycle + 1)
        after_q = conserved(after_fields)
        after = (after_q, flux(after_fields, after_q, 0))
        around = flux(fields, q, 1)
        along = flux(fields, q, 2)
        c = theta_factor(cycle)
        radius = cycle + 0.5
        scale = 0.25 / radius
        sources = (
            None,
            scale * (q[2] * fields[2] + fields[4]),
            -scale * (q[1] * fields[2]),
            None,
            None,
        )
        for f in range(FIELDS):
            own = q[f] * (0.8 - 0.8 * c)
            if sources[f] is not None:
                own = own + sources[f]
            smooth, push = SMOOTH * q[f], HALF_STEP * along[f]
            forward, backward = spread(smooth + push, 1, 1), spread(smooth - push, -1, 1)
            own = own + jnp.where(first_lane, 0.0, forward) + jnp.where(last_lane, 0.0, backward)
            beyond = jnp.where(first_lane, forward, jnp.where(last_lane, backward, 0.0))
            border[f] = border[f] + spread(beyond, 16 * cycle + 1, 1)
            smooth, push = (0.4 * c) * q[f], c * around[f]
            rising, falling = smooth + push, smooth - push
            own = own + jnp.where(not_first_row, spread(rising, 1, 0), 0.0)
            own = own + jnp.where(not_last_row, spread(falling, -1, 0), 0.0)
            own = own + (SMOOTH * after[0][f] - (HALF_STEP * (radius + 1.0) / radius) * after[1][f])
            if before is not None:
                own = own + (SMOOTH * before[0][f] + (HALF_STEP * (radius - 1.0) / radius) * before[1][f])
            up, down = rising[7:8], falling[0:1]
            if f < 4:
                unit = f * NF + cycle
                store(unit, 0, own)
                store(unit, 8, up)
                store(unit, 15, down)
            else:
                packs = half_packs(own)
                store(cycle, 10, packs[0])
                store(cycle, 9, jnp.where(low, down, spread(up, 64, 1)))
                store(NF + cycle, 10, packs[1])
                store(NF + cycle, 9, jnp.where(low, spread(down, 64, 1), up))
        before = (q, radial)
        fields, q, radial = after_fields, after_q, after[1]
    rows = [
        jnp.sum(pltpu.roll(value, 0, 1, stride=2, stride_axis=0), axis=0, keepdims=True) for value in border
    ]
    others = jnp.concatenate(rows[1:], axis=0)
    for unit in range(N_TH):
        store(unit, 14, rows[0])
        store(unit, 16, others)


def in_vmem(value):
    return pltpu.with_memory_space_constraint(value, pltpu.VMEM)


def in_hbm(value):
    return pltpu.with_memory_space_constraint(value, pltpu.HBM)


PARAMS = pltpu.CompilerParams(vmem_limit_bytes=24 << 20)
WHOLE = pl.BlockSpec(memory_space=pltpu.VMEM)


def inner_part(density, velocity, pressure):
    return pl.pallas_call(
        inner_kernel,
        grid=(1,),
        in_specs=[
            pl.BlockSpec((SECTOR, 16, LANES), lambda i: (0, 0, 0)),
            pl.BlockSpec((3, SECTOR, 16, LANES), lambda i: (0, 0, 0, 0)),
            pl.BlockSpec((SECTOR, 16, LANES), lambda i: (0, 0, 0)),
        ],
        out_specs=WHOLE,
        out_shape=pltpu.VMEM((N_TH * SEND_ROWS, LANES), jnp.float32),
        compiler_params=PARAMS,
        cost_estimate=pl.CostEstimate(flops=8 * 1024 * 200, bytes_accessed=600_000, transcendentals=0),
        name="inner_part",
    )(in_hbm(density), in_hbm(velocity), in_hbm(pressure))


def edge_kernel(d_ref, v_ref, p_ref, near_ref, far_ref, columns_ref):
    lane = lanes_of((NR, LANES))
    odd = lax.axis_index("th") % 2 == 1

    def load(f, j):
        return d_ref[j] if f == 0 else (p_ref[j] if f == 4 else v_ref[f - 1, j])

    firsts = jnp.zeros((NR, LANES), jnp.float32)
    lasts = firsts
    for f in range(FIELDS):
        for j in range(SECTOR):
            spot = 16 * f + 2 * j
            value = spread(load(f, j), spot + 1, 1)
            firsts = jnp.where(lane == spot + 1, value, firsts)
            lasts = jnp.where(lane == spot, value, lasts)
        first, last = load(f, 0), load(f, SECTOR - 1)
        near_ref[f] = jnp.where(odd, first, last)
        far_ref[f] = jnp.where(odd, last, first)
    columns_ref[...] = spread(firsts, -1, 1) + spread(lasts, 1, 1)


def edges(density, velocity, pressure):
    rows = pltpu.VMEM((ROW_FIELDS, NR, LANES), jnp.float32)
    return pl.pallas_call(
        edge_kernel,
        in_specs=[WHOLE] * 3,
        out_specs=[WHOLE] * 3,
        out_shape=[rows, rows, pltpu.VMEM((NR, LANES), jnp.float32)],
        compiler_params=PARAMS,
        cost_estimate=pl.CostEstimate(flops=320 * 1024 * 3, bytes_accessed=1_800_000, transcendentals=0),
        name="edges",
    )(in_vmem(density), in_vmem(velocity), in_vmem(pressure))


def axial_terms(both):
    lane = lanes_of(both.shape)
    fields = [both] + [spread(both, -16 * f, 1) for f in range(1, FIELDS)]
    q = conserved(fields)
    along = flux(fields, q, 2)
    push = jnp.where(lane % 2 == 1, HALF_STEP, -HALF_STEP)
    return [SMOOTH * q[f] + push * along[f] for f in range(FIELDS)]


def filter_kernel(r_ref, w_ref, weights_ref, columns_ref, out_ref, up_ref, down_ref):
    shape = (N_TH, SECTOR, LANES)
    row, lane = rows_of(shape), lanes_of(shape)
    starts = [slot(s) * SEND_ROWS for s in range(N_TH)]
    main = jnp.stack([r_ref[a : a + 8, :] for a in starts])
    extra = jnp.stack([r_ref[a + 8 : a + 16, :] for a in starts])
    zero = jnp.zeros(shape, jnp.float32)

    def earlier(value):
        return jnp.concatenate([value[-1:], value[:-1]], axis=0)

    def later(value):
        return jnp.concatenate([value[1:], value[:1]], axis=0)

    main = main + jnp.where(row == 0, earlier(extra), jnp.where(row == 7, later(extra), zero))
    turned = spread(extra, 64, 2)
    top = spread(extra, 6, 1)
    half = jnp.where(row < 4, top, spread(turned, 2, 1))
    half = half + jnp.where(
        row == 0, earlier(spread(turned, 7, 1)), jnp.where(row == 7, later(top), zero)
    )

    def product(high, low, value):
        value = value.reshape(NTH, LANES)
        big = value.astype(jnp.bfloat16)
        small = (value - big.astype(jnp.float32)).astype(jnp.bfloat16)
        out = jnp.dot(high, big, preferred_element_type=jnp.float32)
        out = out + jnp.dot(high, small, preferred_element_type=jnp.float32)
        out = out + jnp.dot(low, big, preferred_element_type=jnp.float32)
        return out.reshape(shape)

    main = product(w_ref[0], w_ref[1], main)
    half = product(w_ref[2], w_ref[3], half)
    packed = jnp.where(lane < 64, half, spread(spread(half, 64, 2), 4, 1))
    sums = [jnp.zeros((SECTOR, LANES), jnp.float32) for _ in range(FIELDS)]
    for s in range(N_TH):
        base, start = slot(s) * BACK_ROWS, starts[s]
        out_ref[base : base + 8, :] = main[s]
        out_ref[base + 8 : base + 12, :] = packed[s, :4]
        weights = weights_ref[SECTOR * s : SECTOR * (s + 1), :]
        for f, place in enumerate((14, 16, 17, 18, 19)):
            sums[f] = sums[f] + weights * r_ref[start + place : start + place + 1, :]
    first = lanes_of((SECTOR, LANES)) % 16 < 2
    terms = jnp.zeros((SECTOR, LANES), jnp.float32)
    for f in range(FIELDS):
        for shift in (2, 4, 8):
            sums[f] = sums[f] + spread(sums[f], -shift, 1)
        terms = terms + spread(jnp.where(first, sums[f], 0.0), 2 * f, 1)
    columns = columns_ref[...]
    up, down = two_halves(columns[: NR // 2], columns[NR // 2 :])
    for target, value in ((up_ref, up), (down_ref, down)):
        target[:SECTOR, :] = terms
        target[SECTOR:PACK_ROWS, :] = value


def two_halves(upper, lower):
    odd = lanes_of(upper.shape) % 2 == 1
    return jnp.where(odd, upper, spread(lower, -1, 1)), jnp.where(odd, spread(upper, 1, 1), lower)


def from_halves(odd_lanes, even_lanes):
    odd = lanes_of(odd_lanes.shape) % 2 == 1
    upper = jnp.where(odd, odd_lanes, spread(even_lanes, -1, 1))
    lower = jnp.where(odd, spread(odd_lanes, 1, 1), even_lanes)
    return upper, lower


def filtered(received, matrices, weights, columns):
    up = pltpu.VMEM((PACK_ROWS + UP_ROWS, LANES), jnp.float32)
    down = pltpu.VMEM((PACK_ROWS + DOWN_ROWS, LANES), jnp.float32)
    return pl.pallas_call(
        filter_kernel,
        in_specs=[WHOLE] * 4,
        out_specs=[WHOLE] * 3,
        out_shape=[pltpu.VMEM((N_TH * BACK_ROWS, LANES), jnp.float32), up, down],
        compiler_params=PARAMS,
        cost_estimate=pl.CostEstimate(flops=6 * 256 * 256 * 256, bytes_accessed=1_200_000, transcendentals=0),
        name="filtered",
    )(*[in_vmem(value) for value in (received, matrices, weights, columns)])


def theta_terms(fields, q, c):
    around = flux(fields, q, 1)
    smooth = [(0.4 * c) * part for part in q]
    push = [c * part for part in around]
    return [a + b for a, b in zip(smooth, push)], [a - b for a, b in zip(smooth, push)]


def outer_kernel(
    high_ref, low_ref, table_ref, d_ref, v_ref, p_ref, out_ref, w_ref, weights_ref, rising_ref, done
):
    th = lax.axis_index("th")
    cycle = th % NF
    half = jnp.where(th < 2 * NF, cycle, jnp.where(th < 2 * NF + 2 * FIELDS, NF, 0))
    copies = [
        pltpu.make_async_copy(table.at[place], w_ref.at[2 * k + n], done.at[2 * k + n])
        for k, place in enumerate((cycle, half))
        for n, table in enumerate((high_ref, low_ref))
    ]
    first = pl.multiple_of((N_TH - 1 - th) * SECTOR, SECTOR)
    copies.append(
        pltpu.make_async_copy(table_ref.at[pl.ds(first, N_TH * SECTOR), :], weights_ref, done.at[4])
    )
    for copy in copies:
        copy.start()
    shape = (NR, LANES)
    lane, row = lanes_of(shape)[NF:], rows_of(shape)
    radius = row.astype(jnp.float32) + 0.5
    inverse = (1.0 / radius)[NF:]
    c = (theta_factor(0) * 0.5) * inverse
    first_lane, last_lane = lane == 0, lane == LANES - 1
    last_row = row == NR - 1
    own_scale, source_scale = 0.8 - 0.8 * c, 0.25 * inverse
    push_scale = HALF_STEP * radius
    for f in range(FIELDS):
        rising_ref[f] = jnp.zeros((NR - NF, LANES), jnp.float32)

    def rows_at(f, j):
        return pl.ds(pl.multiple_of((f * SECTOR + j) * OUTER, NF), OUTER)

    def step(j, carry):
        every = (d_ref[j], v_ref[0, j], v_ref[1, j], v_ref[2, j], p_ref[j])
        every_q = conserved(every)
        radial = flux(every, every_q, 0)
        fields, q = [part[NF:] for part in every], [part[NF:] for part in every_q]
        along = flux(fields, q, 2)
        rising, falling = theta_terms(fields, q, c)
        sources = (
            None,
            source_scale * (q[2] * fields[2] + fields[4]),
            -source_scale * (q[1] * fields[2]),
            None,
            None,
        )
        for f in range(FIELDS):
            own = q[f] * own_scale
            if sources[f] is not None:
                own = own + sources[f]
            smooth, push = SMOOTH * every_q[f], HALF_STEP * along[f]
            near = smooth[NF:]
            own = own + jnp.where(first_lane, 0.0, spread(near + push, 1, 1))
            own = own + jnp.where(last_lane, 0.0, spread(near - push, LANES - 1, 1))
            push = push_scale * radial[f]
            ghost = push + HALF_STEP * radial[f]
            smooth_ahead = jnp.where(last_row, smooth, spread(smooth, NR - 1, 0))
            push_ahead = jnp.where(last_row, ghost, spread(push, NR - 1, 0))
            own = own + (smooth_ahead + spread(smooth, 1, 0))[NF:]
            own = own + inverse * (spread(push, 1, 0) - push_ahead)[NF:]
            out_ref[rows_at(f, j), :] = own + rising_ref[f]
            rising_ref[f] = rising[f]

        @pl.when(j > 0)
        def _():
            for f in range(FIELDS):
                out_ref[rows_at(f, j - 1), :] = out_ref[rows_at(f, j - 1), :] + falling[f]

        return carry

    lax.fori_loop(0, SECTOR, step, 0)
    for copy in copies:
        copy.wait()


def outer_part(high, low, table, density, velocity, pressure):
    return pl.pallas_call(
        outer_kernel,
        in_specs=[pl.BlockSpec(memory_space=pl.ANY)] * 3 + [WHOLE] * 3,
        out_specs=[WHOLE] * 3,
        out_shape=[
            pltpu.VMEM((BLOCK_ROWS, LANES), jnp.float32),
            pltpu.VMEM((4, NTH, NTH), jnp.bfloat16),
            pltpu.VMEM((N_TH * SECTOR, LANES), jnp.float32),
        ],
        scratch_shapes=[
            pltpu.VMEM((FIELDS, NR - NF, LANES), jnp.float32),
            pltpu.SemaphoreType.DMA((5,)),
        ],
        compiler_params=PARAMS,
        cost_estimate=pl.CostEstimate(flops=64 * 1024 * 250, bytes_accessed=3_000_000, transcendentals=0),
        name="outer_part",
    )(
        *[in_hbm(value) for value in (high, low, table)],
        *[in_vmem(value) for value in (density, velocity, pressure)],
    )


def finish_kernel(
    r_ref, before_ref, after_ref, rest_ref, side_ref, back_ref, out_ref, buffer, rows_ref, done
):
    arrivals = [
        pltpu.make_async_copy(
            value.at[pl.ds(0, FIELDS), pl.ds(NF, NR - NF), :], rows_ref.at[n], done.at[SECTOR + 1 + n]
        )
        for n, value in enumerate((side_ref, back_ref))
    ]
    for copy in arrivals:
        copy.start()
    before, after = before_ref[:PACK_ROWS, :], after_ref[:PACK_ROWS, :]
    upper, lower = from_halves(before[SECTOR:], after[SECTOR:])
    terms = axial_terms(jnp.concatenate([upper, lower], axis=0)[NF:])
    shape = (SECTOR, LANES)
    lane = lanes_of(shape)
    ends = (lane == 0) | (lane == LANES - 1)
    border = jnp.where(lane % 2 == 1, before[:SECTOR], after[:SECTOR])
    low_half = lanes_of((4, LANES)) < 64
    far_lane = lanes_of((NR - NF, LANES))
    far_ends = (far_lane == 0) | (far_lane == LANES - 1)

    def outer(j):
        rows = pl.ds(NF, NR - NF)
        return pltpu.make_async_copy(buffer.at[:, j, rows, :], out_ref.at[:, j, rows, :], done.at[j])

    def write_outer(j, more):
        for f in range(FIELDS):
            beyond = jnp.where(far_ends, spread(terms[f], LANES - 1 - 2 * j, 1), 0.0)
            if more is not None:
                beyond = beyond + more[f]
            first = (f * SECTOR + j) * OUTER
            buffer[f, j, NF:, :] = rest_ref[first : first + OUTER, :] + beyond
        outer(j).start()

    for j in range(1, SECTOR - 1):
        write_outer(j, None)

    tiles = buffer.reshape(FIELDS * SECTOR * NR, LANES)

    def joined(unit_a, unit_b):
        start_a, start_b = slot(unit_a) * BACK_ROWS + 8, slot(unit_b) * BACK_ROWS + 8
        a, b = r_ref[start_a : start_a + 4, :], r_ref[start_b : start_b + 4, :]
        top = jnp.where(low_half, a, spread(b, 64, 1))
        bottom = jnp.where(low_half, spread(a, 64, 1), b)
        return jnp.concatenate([top, bottom], axis=0)

    for f in range(FIELDS):
        for cycle in range(NF):
            if f < 4:
                start = slot(f * NF + cycle) * BACK_ROWS
                tile = r_ref[start : start + 8, :]
            else:
                tile = joined(cycle, NF + cycle)
            if cycle == 0:
                tile = tile + joined(16 + 2 * f, 17 + 2 * f)
            tile = tile + jnp.where(ends, spread(border, -(16 * cycle + 2 * f + 1), 1), 0.0)
            tiles[pl.ds(f * SECTOR * NR + cycle, SECTOR, stride=NR), :] = tile
    rows = pl.ds(0, NF)
    inner = pltpu.make_async_copy(buffer.at[:, :, rows, :], out_ref.at[:, :, rows, :], done.at[SECTOR])
    inner.start()
    for copy in arrivals:
        copy.wait()
    c = (theta_factor(0) * 0.5) / (rows_of((NR, LANES))[NF:].astype(jnp.float32) + 0.5)
    odd = lax.axis_index("th") % 2 == 1
    side = [rows_ref[0, f] for f in range(FIELDS)]
    back = [rows_ref[1, f] for f in range(FIELDS)]
    below = [jnp.where(odd, a, b) for a, b in zip(side, back)]
    above = [jnp.where(odd, b, a) for a, b in zip(side, back)]
    write_outer(0, theta_terms(below, conserved(below), c)[0])
    write_outer(SECTOR - 1, theta_terms(above, conserved(above), c)[1])
    for j in range(SECTOR):
        outer(j).wait()
    inner.wait()


def finish(received, before, after, rest, side, back):
    block = (FIELDS, SECTOR, NR, LANES)
    return pl.pallas_call(
        finish_kernel,
        in_specs=[WHOLE] * 4 + [pl.BlockSpec(memory_space=pl.ANY)] * 2,
        out_specs=pl.BlockSpec(memory_space=pl.ANY),
        out_shape=jax.ShapeDtypeStruct(block, jnp.float32),
        scratch_shapes=[
            pltpu.VMEM(block, jnp.float32),
            pltpu.VMEM((2, FIELDS, NR - NF, LANES), jnp.float32),
            pltpu.SemaphoreType.DMA((SECTOR + 3,)),
        ],
        compiler_params=PARAMS,
        cost_estimate=pl.CostEstimate(flops=400 * 1024, bytes_accessed=3_000_000, transcendentals=0),
        name="finish",
    )(
        *[in_vmem(value) for value in (received, before, after, rest)],
        in_hbm(side),
        in_hbm(back),
    )


def pairs(size, offset):
    return [(i, (((i - offset) ^ 1) + offset) % size) for i in range(size)]


def transposed(value, rows):
    value = value.reshape(N_TH, rows // 4, 4, LANES)
    group = [(FIRST + k) % N_TH for k in range(N_TH)]
    value = lax.all_to_all(value, "th", 0, 0, tiled=True, axis_index_groups=[group])
    return value.reshape(N_TH * rows, LANES)


def per_device(density, velocity, pressure):
    high, low = filter_matrices()
    high, low = jnp.asarray(high), jnp.asarray(low)
    table = jnp.asarray(edge_weights())
    sent = inner_part(density, velocity, pressure)
    received = transposed(sent, SEND_ROWS)

    near_row, far_row, columns = edges(density, velocity, pressure)
    th_far = lax.ppermute(far_row, "th", pairs(N_TH, 1))
    th_near = lax.ppermute(near_row, "th", pairs(N_TH, 0))

    rest, matrices, weights = outer_part(high, low, table, density, velocity, pressure)
    back, up, down = filtered(received, matrices, weights, columns)
    up, down, th_far, th_near = lax.optimization_barrier((up, down, th_far, th_near))
    returned = transposed(back, BACK_ROWS)
    size = lax.axis_size("gz")
    before = lax.ppermute(up, "gz", [(i, (i + 1) % size) for i in range(size)])
    after = lax.ppermute(down, "gz", [(i, (i - 1) % size) for i in range(size)])
    return finish(returned, before, after, rest, th_near, th_far)


def solution(mesh):
    in_specs = (P("th", None, "gz"), P(None, "th", None, "gz"), P("th", None, "gz"))
    out_specs = P(None, "th", None, "gz")
    return jax.shard_map(
        per_device, mesh=mesh, in_specs=in_specs, out_specs=out_specs, check_vma=False
    )
```

```python
import math

import jax
import jax.numpy as jnp
import ml_dtypes
import numpy as np
from jax import lax
from jax.experimental import pallas as pl
from jax.experimental.pallas import tpu as pltpu
from jax.sharding import PartitionSpec as P

NTH = 256
NR = 64
NF = 8
N_TH = 32
SECTOR = NTH // N_TH
LANES = 128
FIELDS = 5
SEND_ROWS = 20
BACK_ROWS = 12
OUTER = NR - NF
BLOCK_ROWS = FIELDS * SECTOR * OUTER
PACK_ROWS = SECTOR + NR // 2
UP_ROWS, DOWN_ROWS = 0, 0
ORDER = [(23 + n) % N_TH for n in range(N_TH)]
BACK_ORDER = [(16 + n) % N_TH for n in range(N_TH)]
ROW_FIELDS = 11

HALF_STEP = 0.125
SMOOTH = 0.05


def theta_factor(cycle):
    return 0.25 / (2.0 * (2.0 * math.pi / NTH) * (cycle + 0.5))


def filter_rows():
    modes = np.arange(NTH)
    folded = np.minimum(modes, NTH - modes)
    waves = np.cos(2.0 * math.pi * (modes[:, None] * modes[None, :] % NTH) / NTH)
    rows = []
    for cycle in range(NF):
        keep = 2 * (NF + 1) * folded <= NTH * (cycle + 1)
        rows.append(waves[:, keep].sum(axis=1) / NTH)
    return np.stack(rows)


def filter_matrices():
    rows = filter_rows()
    index = (np.arange(NTH)[:, None] - np.arange(NTH)[None, :]) % NTH
    full = np.concatenate([rows[:, index], rows[:1, (index + NTH // 2) % NTH]]).astype(np.float32)
    high = full.astype(ml_dtypes.bfloat16)
    low = (full - high.astype(np.float32)).astype(ml_dtypes.bfloat16)
    return high, low


def edge_weights():
    rows = filter_rows()
    table = np.zeros((2 * N_TH, SECTOR, LANES), np.float32)
    for row in range(2 * N_TH - 1):
        apart = (N_TH - 1 - row) * SECTOR
        index = (apart + np.arange(SECTOR)[:, None] - np.arange(SECTOR)[None, :]) % NTH
        block = np.repeat(rows[:, index].transpose(1, 0, 2)[..., None], 2, axis=3)
        table[row] = block.reshape(SECTOR, LANES)
    return table.reshape(2 * N_TH * SECTOR, LANES)


def conserved(fields):
    rho, ur, ut, uz, p = fields
    qr, qt, qz = rho * ur, rho * ut, rho * uz
    energy = p * 2.5 + 0.5 * (qr * ur + qt * ut + qz * uz)
    return rho, qr, qt, qz, energy


def flux(fields, q, direction):
    p = fields[4]
    speed = fields[1 + direction]
    moving = q[1 + direction]
    parts = [moving, moving * fields[1], moving * fields[2], moving * fields[3], speed * (q[4] + p)]
    parts[1 + direction] = parts[1 + direction] + p
    return parts


def slot(sector, order):
    return order.index(sector)


def lanes_of(shape):
    return lax.broadcasted_iota(jnp.int32, shape, len(shape) - 1)


def rows_of(shape):
    return lax.broadcasted_iota(jnp.int32, shape, len(shape) - 2)


def spread(value, shift, axis):
    size = value.shape[axis]
    return pltpu.roll(value, shift % size, axis)


def half_packs(tile):
    turned = spread(tile, 64, 1)
    low = lanes_of((SECTOR, LANES)) < 64
    first = jnp.where(low, tile, spread(turned, 4, 0))
    second = jnp.where(low, turned, spread(tile, 4, 0))
    return first[:4], second[:4]


def inner_kernel(d_ref, v_ref, p_ref, out_ref):
    size = 16 * SECTOR
    d_rows, v_rows, p_rows = (
        d_ref.reshape(size, LANES), v_ref.reshape(3 * size, LANES), p_ref.reshape(size, LANES)
    )

    def load(cycle):
        def rows(ref, first):
            return ref[pl.ds(first + cycle, SECTOR, stride=16), :]

        return (rows(d_rows, 0), *[rows(v_rows, n * size) for n in range(3)], rows(p_rows, 0))

    def store(unit, row, value):
        start = slot(unit, ORDER) * SEND_ROWS + row
        out_ref[start : start + value.shape[0], :] = value

    shape = (SECTOR, LANES)
    lane, row = lanes_of(shape), rows_of(shape)
    first_lane, last_lane = lane == 0, lane == LANES - 1
    not_first_row, not_last_row = row > 0, row < SECTOR - 1
    low = lanes_of((1, LANES)) < 64
    for unit in range(16, N_TH):
        store(unit, 9, jnp.zeros((5, LANES), jnp.float32))

    before = None
    fields = load(0)
    q = conserved(fields)
    radial = flux(fields, q, 0)
    for f in range(FIELDS):
        sign = -1.0 if f in (1, 2) else 1.0
        mirrored = sign * (SMOOTH * q[f] + HALF_STEP * radial[f])
        for half, pack in enumerate(half_packs(mirrored)):
            store(16 + 2 * f + half, 10, pack)
    border = [jnp.zeros(shape, jnp.float32) for _ in range(FIELDS)]
    for cycle in range(NF):
        after_fields = load(cycle + 1)
        after_q = conserved(after_fields)
        after = (after_q, flux(after_fields, after_q, 0))
        around = flux(fields, q, 1)
        along = flux(fields, q, 2)
        c = theta_factor(cycle)
        radius = cycle + 0.5
        scale = 0.25 / radius
        sources = (
            None,
            scale * (q[2] * fields[2] + fields[4]),
            -scale * (q[1] * fields[2]),
            None,
            None,
        )
        for f in range(FIELDS):
            own = q[f] * (0.8 - 0.8 * c)
            if sources[f] is not None:
                own = own + sources[f]
            smooth, push = SMOOTH * q[f], HALF_STEP * along[f]
            forward, backward = spread(smooth + push, 1, 1), spread(smooth - push, -1, 1)
            own = own + jnp.where(first_lane, 0.0, forward) + jnp.where(last_lane, 0.0, backward)
            beyond = jnp.where(first_lane, forward, jnp.where(last_lane, backward, 0.0))
            border[f] = border[f] + spread(beyond, 16 * cycle + 1, 1)
            smooth, push = (0.4 * c) * q[f], c * around[f]
            rising, falling = smooth + push, smooth - push
            own = own + jnp.where(not_first_row, spread(rising, 1, 0), 0.0)
            own = own + jnp.where(not_last_row, spread(falling, -1, 0), 0.0)
            own = own + (SMOOTH * after[0][f] - (HALF_STEP * (radius + 1.0) / radius) * after[1][f])
            if before is not None:
                own = own + (SMOOTH * before[0][f] + (HALF_STEP * (radius - 1.0) / radius) * before[1][f])
            up, down = rising[7:8], falling[0:1]
            if f < 4:
                unit = f * NF + cycle
                store(unit, 0, own)
                store(unit, 8, up)
                store(unit, 15, down)
            else:
                packs = half_packs(own)
                store(cycle, 10, packs[0])
                store(cycle, 9, jnp.where(low, down, spread(up, 64, 1)))
                store(NF + cycle, 10, packs[1])
                store(NF + cycle, 9, jnp.where(low, spread(down, 64, 1), up))
        before = (q, radial)
        fields, q, radial = after_fields, after_q, after[1]
    rows = [
        jnp.sum(pltpu.roll(value, 0, 1, stride=2, stride_axis=0), axis=0, keepdims=True) for value in border
    ]
    others = jnp.concatenate(rows[1:], axis=0)
    for unit in range(N_TH):
        store(unit, 14, rows[0])
        store(unit, 16, others)


def in_vmem(value):
    return pltpu.with_memory_space_constraint(value, pltpu.VMEM)


def in_hbm(value):
    return pltpu.with_memory_space_constraint(value, pltpu.HBM)


PARAMS = pltpu.CompilerParams(vmem_limit_bytes=24 << 20)
WHOLE = pl.BlockSpec(memory_space=pltpu.VMEM)


def inner_part(density, velocity, pressure):
    return pl.pallas_call(
        inner_kernel,
        grid=(1,),
        in_specs=[
            pl.BlockSpec((SECTOR, 16, LANES), lambda i: (0, 0, 0)),
            pl.BlockSpec((3, SECTOR, 16, LANES), lambda i: (0, 0, 0, 0)),
            pl.BlockSpec((SECTOR, 16, LANES), lambda i: (0, 0, 0)),
        ],
        out_specs=WHOLE,
        out_shape=pltpu.VMEM((N_TH * SEND_ROWS, LANES), jnp.float32),
        compiler_params=PARAMS,
        cost_estimate=pl.CostEstimate(flops=8 * 1024 * 200, bytes_accessed=600_000, transcendentals=0),
        name="inner_part",
    )(in_hbm(density), in_hbm(velocity), in_hbm(pressure))


def edge_kernel(d_ref, v_ref, p_ref, near_ref, far_ref, columns_ref):
    lane = lanes_of((NR, LANES))
    odd = lax.axis_index("th") % 2 == 1

    def load(f, j):
        return d_ref[j] if f == 0 else (p_ref[j] if f == 4 else v_ref[f - 1, j])

    firsts = jnp.zeros((NR, LANES), jnp.float32)
    lasts = firsts
    for f in range(FIELDS):
        for j in range(SECTOR):
            spot = 16 * f + 2 * j
            value = spread(load(f, j), spot + 1, 1)
            firsts = jnp.where(lane == spot + 1, value, firsts)
            lasts = jnp.where(lane == spot, value, lasts)
        first, last = load(f, 0), load(f, SECTOR - 1)
        near_ref[f] = jnp.where(odd, first, last)
        far_ref[f] = jnp.where(odd, last, first)
    columns_ref[...] = spread(firsts, -1, 1) + spread(lasts, 1, 1)


def edges(density, velocity, pressure):
    rows = pltpu.VMEM((ROW_FIELDS, NR, LANES), jnp.float32)
    return pl.pallas_call(
        edge_kernel,
        in_specs=[WHOLE] * 3,
        out_specs=[WHOLE] * 3,
        out_shape=[rows, rows, pltpu.VMEM((NR, LANES), jnp.float32)],
        compiler_params=PARAMS,
        cost_estimate=pl.CostEstimate(flops=320 * 1024 * 3, bytes_accessed=1_800_000, transcendentals=0),
        name="edges",
    )(in_vmem(density), in_vmem(velocity), in_vmem(pressure))


def axial_terms(both):
    lane = lanes_of(both.shape)
    fields = [both] + [spread(both, -16 * f, 1) for f in range(1, FIELDS)]
    q = conserved(fields)
    along = flux(fields, q, 2)
    push = jnp.where(lane % 2 == 1, HALF_STEP, -HALF_STEP)
    return [SMOOTH * q[f] + push * along[f] for f in range(FIELDS)]


def filter_kernel(r_ref, w_ref, weights_ref, columns_ref, out_ref, up_ref, down_ref):
    shape = (N_TH, SECTOR, LANES)
    row, lane = rows_of(shape), lanes_of(shape)
    starts = [slot(s, ORDER) * SEND_ROWS for s in range(N_TH)]
    main = jnp.stack([r_ref[a : a + 8, :] for a in starts])
    extra = jnp.stack([r_ref[a + 8 : a + 16, :] for a in starts])
    zero = jnp.zeros(shape, jnp.float32)

    def earlier(value):
        return jnp.concatenate([value[-1:], value[:-1]], axis=0)

    def later(value):
        return jnp.concatenate([value[1:], value[:1]], axis=0)

    main = main + jnp.where(row == 0, earlier(extra), jnp.where(row == 7, later(extra), zero))
    turned = spread(extra, 64, 2)
    top = spread(extra, 6, 1)
    half = jnp.where(row < 4, top, spread(turned, 2, 1))
    half = half + jnp.where(
        row == 0, earlier(spread(turned, 7, 1)), jnp.where(row == 7, later(top), zero)
    )

    def product(high, low, value):
        value = value.reshape(NTH, LANES)
        big = value.astype(jnp.bfloat16)
        small = (value - big.astype(jnp.float32)).astype(jnp.bfloat16)
        out = jnp.dot(high, big, preferred_element_type=jnp.float32)
        out = out + jnp.dot(high, small, preferred_element_type=jnp.float32)
        out = out + jnp.dot(low, big, preferred_element_type=jnp.float32)
        return out.reshape(shape)

    main = product(w_ref[0], w_ref[1], main)
    half = product(w_ref[2], w_ref[3], half)
    packed = jnp.where(lane < 64, half, spread(spread(half, 64, 2), 4, 1))
    sums = [jnp.zeros((SECTOR, LANES), jnp.float32) for _ in range(FIELDS)]
    for s in range(N_TH):
        base, start = slot(s, BACK_ORDER) * BACK_ROWS, starts[s]
        out_ref[base : base + 8, :] = main[s]
        out_ref[base + 8 : base + 12, :] = packed[s, :4]
        weights = weights_ref[SECTOR * s : SECTOR * (s + 1), :]
        for f, place in enumerate((14, 16, 17, 18, 19)):
            sums[f] = sums[f] + weights * r_ref[start + place : start + place + 1, :]
    first = lanes_of((SECTOR, LANES)) % 16 < 2
    terms = jnp.zeros((SECTOR, LANES), jnp.float32)
    for f in range(FIELDS):
        for shift in (2, 4, 8):
            sums[f] = sums[f] + spread(sums[f], -shift, 1)
        terms = terms + spread(jnp.where(first, sums[f], 0.0), 2 * f, 1)
    columns = columns_ref[...]
    up, down = two_halves(columns[: NR // 2], columns[NR // 2 :])
    for target, value in ((up_ref, up), (down_ref, down)):
        target[:SECTOR, :] = terms
        target[SECTOR:PACK_ROWS, :] = value


def two_halves(upper, lower):
    odd = lanes_of(upper.shape) % 2 == 1
    return jnp.where(odd, upper, spread(lower, -1, 1)), jnp.where(odd, spread(upper, 1, 1), lower)


def from_halves(odd_lanes, even_lanes):
    odd = lanes_of(odd_lanes.shape) % 2 == 1
    upper = jnp.where(odd, odd_lanes, spread(even_lanes, -1, 1))
    lower = jnp.where(odd, spread(odd_lanes, 1, 1), even_lanes)
    return upper, lower


def filtered(received, matrices, weights, columns):
    up = pltpu.VMEM((PACK_ROWS + UP_ROWS, LANES), jnp.float32)
    down = pltpu.VMEM((PACK_ROWS + DOWN_ROWS, LANES), jnp.float32)
    return pl.pallas_call(
        filter_kernel,
        in_specs=[WHOLE] * 4,
        out_specs=[WHOLE] * 3,
        out_shape=[pltpu.VMEM((N_TH * BACK_ROWS, LANES), jnp.float32), up, down],
        compiler_params=PARAMS,
        cost_estimate=pl.CostEstimate(flops=6 * 256 * 256 * 256, bytes_accessed=1_200_000, transcendentals=0),
        name="filtered",
    )(*[in_vmem(value) for value in (received, matrices, weights, columns)])


def theta_terms(fields, q, c):
    around = flux(fields, q, 1)
    smooth = [(0.4 * c) * part for part in q]
    push = [c * part for part in around]
    return [a + b for a, b in zip(smooth, push)], [a - b for a, b in zip(smooth, push)]


def outer_kernel(
    high_ref, low_ref, table_ref, d_ref, v_ref, p_ref, out_ref, w_ref, weights_ref, rising_ref, done
):
    th = lax.axis_index("th")
    cycle = th % NF
    half = jnp.where(th < 2 * NF, cycle, jnp.where(th < 2 * NF + 2 * FIELDS, NF, 0))
    copies = [
        pltpu.make_async_copy(table.at[place], w_ref.at[2 * k + n], done.at[2 * k + n])
        for k, place in enumerate((cycle, half))
        for n, table in enumerate((high_ref, low_ref))
    ]
    first = pl.multiple_of((N_TH - 1 - th) * SECTOR, SECTOR)
    copies.append(
        pltpu.make_async_copy(table_ref.at[pl.ds(first, N_TH * SECTOR), :], weights_ref, done.at[4])
    )
    for copy in copies:
        copy.start()
    shape = (NR, LANES)
    lane, row = lanes_of(shape)[NF:], rows_of(shape)
    radius = row.astype(jnp.float32) + 0.5
    inverse = (1.0 / radius)[NF:]
    c = (theta_factor(0) * 0.5) * inverse
    first_lane, last_lane = lane == 0, lane == LANES - 1
    last_row = row == NR - 1
    own_scale, source_scale = 0.8 - 0.8 * c, 0.25 * inverse
    push_scale = HALF_STEP * radius
    for f in range(FIELDS):
        rising_ref[f] = jnp.zeros((NR - NF, LANES), jnp.float32)

    def rows_at(f, j):
        return pl.ds(pl.multiple_of((f * SECTOR + j) * OUTER, NF), OUTER)

    def step(j, carry):
        every = (d_ref[j], v_ref[0, j], v_ref[1, j], v_ref[2, j], p_ref[j])
        every_q = conserved(every)
        radial = flux(every, every_q, 0)
        fields, q = [part[NF:] for part in every], [part[NF:] for part in every_q]
        along = flux(fields, q, 2)
        rising, falling = theta_terms(fields, q, c)
        sources = (
            None,
            source_scale * (q[2] * fields[2] + fields[4]),
            -source_scale * (q[1] * fields[2]),
            None,
            None,
        )
        for f in range(FIELDS):
            own = q[f] * own_scale
            if sources[f] is not None:
                own = own + sources[f]
            smooth, push = SMOOTH * every_q[f], HALF_STEP * along[f]
            near = smooth[NF:]
            own = own + jnp.where(first_lane, 0.0, spread(near + push, 1, 1))
            own = own + jnp.where(last_lane, 0.0, spread(near - push, LANES - 1, 1))
            push = push_scale * radial[f]
            ghost = push + HALF_STEP * radial[f]
            smooth_ahead = jnp.where(last_row, smooth, spread(smooth, NR - 1, 0))
            push_ahead = jnp.where(last_row, ghost, spread(push, NR - 1, 0))
            own = own + (smooth_ahead + spread(smooth, 1, 0))[NF:]
            own = own + inverse * (spread(push, 1, 0) - push_ahead)[NF:]
            out_ref[rows_at(f, j), :] = own + rising_ref[f]
            rising_ref[f] = rising[f]

        @pl.when(j > 0)
        def _():
            for f in range(FIELDS):
                out_ref[rows_at(f, j - 1), :] = out_ref[rows_at(f, j - 1), :] + falling[f]

        return carry

    lax.fori_loop(0, SECTOR, step, 0)
    for copy in copies:
        copy.wait()


def outer_part(high, low, table, density, velocity, pressure):
    return pl.pallas_call(
        outer_kernel,
        in_specs=[pl.BlockSpec(memory_space=pl.ANY)] * 3 + [WHOLE] * 3,
        out_specs=[WHOLE] * 3,
        out_shape=[
            pltpu.VMEM((BLOCK_ROWS, LANES), jnp.float32),
            pltpu.VMEM((4, NTH, NTH), jnp.bfloat16),
            pltpu.VMEM((N_TH * SECTOR, LANES), jnp.float32),
        ],
        scratch_shapes=[
            pltpu.VMEM((FIELDS, NR - NF, LANES), jnp.float32),
            pltpu.SemaphoreType.DMA((5,)),
        ],
        compiler_params=PARAMS,
        cost_estimate=pl.CostEstimate(flops=64 * 1024 * 250, bytes_accessed=3_000_000, transcendentals=0),
        name="outer_part",
    )(
        *[in_hbm(value) for value in (high, low, table)],
        *[in_vmem(value) for value in (density, velocity, pressure)],
    )


def finish_kernel(
    r_ref, before_ref, after_ref, rest_ref, side_ref, back_ref, out_ref, buffer, rows_ref, done
):
    arrivals = [
        pltpu.make_async_copy(
            value.at[pl.ds(0, FIELDS), pl.ds(NF, NR - NF), :], rows_ref.at[n], done.at[SECTOR + 1 + n]
        )
        for n, value in enumerate((side_ref, back_ref))
    ]
    for copy in arrivals:
        copy.start()
    before, after = before_ref[:PACK_ROWS, :], after_ref[:PACK_ROWS, :]
    upper, lower = from_halves(before[SECTOR:], after[SECTOR:])
    terms = axial_terms(jnp.concatenate([upper, lower], axis=0)[NF:])
    shape = (SECTOR, LANES)
    lane = lanes_of(shape)
    ends = (lane == 0) | (lane == LANES - 1)
    border = jnp.where(lane % 2 == 1, before[:SECTOR], after[:SECTOR])
    low_half = lanes_of((4, LANES)) < 64
    far_lane = lanes_of((NR - NF, LANES))
    far_ends = (far_lane == 0) | (far_lane == LANES - 1)

    def outer(j):
        rows = pl.ds(NF, NR - NF)
        return pltpu.make_async_copy(buffer.at[:, j, rows, :], out_ref.at[:, j, rows, :], done.at[j])

    def write_outer(j, more):
        for f in range(FIELDS):
            beyond = jnp.where(far_ends, spread(terms[f], LANES - 1 - 2 * j, 1), 0.0)
            if more is not None:
                beyond = beyond + more[f]
            first = (f * SECTOR + j) * OUTER
            buffer[f, j, NF:, :] = rest_ref[first : first + OUTER, :] + beyond
        outer(j).start()

    for j in range(1, SECTOR - 1):
        write_outer(j, None)

    tiles = buffer.reshape(FIELDS * SECTOR * NR, LANES)

    def joined(unit_a, unit_b):
        start_a, start_b = (slot(unit, BACK_ORDER) * BACK_ROWS + 8 for unit in (unit_a, unit_b))
        a, b = r_ref[start_a : start_a + 4, :], r_ref[start_b : start_b + 4, :]
        top = jnp.where(low_half, a, spread(b, 64, 1))
        bottom = jnp.where(low_half, spread(a, 64, 1), b)
        return jnp.concatenate([top, bottom], axis=0)

    for f in range(FIELDS):
        for cycle in range(NF):
            if f < 4:
                start = slot(f * NF + cycle, BACK_ORDER) * BACK_ROWS
                tile = r_ref[start : start + 8, :]
            else:
                tile = joined(cycle, NF + cycle)
            if cycle == 0:
                tile = tile + joined(16 + 2 * f, 17 + 2 * f)
            tile = tile + jnp.where(ends, spread(border, -(16 * cycle + 2 * f + 1), 1), 0.0)
            tiles[pl.ds(f * SECTOR * NR + cycle, SECTOR, stride=NR), :] = tile
    rows = pl.ds(0, NF)
    inner = pltpu.make_async_copy(buffer.at[:, :, rows, :], out_ref.at[:, :, rows, :], done.at[SECTOR])
    inner.start()
    for copy in arrivals:
        copy.wait()
    c = (theta_factor(0) * 0.5) / (rows_of((NR, LANES))[NF:].astype(jnp.float32) + 0.5)
    odd = lax.axis_index("th") % 2 == 1
    side = [rows_ref[0, f] for f in range(FIELDS)]
    back = [rows_ref[1, f] for f in range(FIELDS)]
    below = [jnp.where(odd, a, b) for a, b in zip(side, back)]
    above = [jnp.where(odd, b, a) for a, b in zip(side, back)]
    write_outer(0, theta_terms(below, conserved(below), c)[0])
    write_outer(SECTOR - 1, theta_terms(above, conserved(above), c)[1])
    for j in range(SECTOR):
        outer(j).wait()
    inner.wait()


def finish(received, before, after, rest, side, back):
    block = (FIELDS, SECTOR, NR, LANES)
    return pl.pallas_call(
        finish_kernel,
        in_specs=[WHOLE] * 4 + [pl.BlockSpec(memory_space=pl.ANY)] * 2,
        out_specs=pl.BlockSpec(memory_space=pl.ANY),
        out_shape=jax.ShapeDtypeStruct(block, jnp.float32),
        scratch_shapes=[
            pltpu.VMEM(block, jnp.float32),
            pltpu.VMEM((2, FIELDS, NR - NF, LANES), jnp.float32),
            pltpu.SemaphoreType.DMA((SECTOR + 3,)),
        ],
        compiler_params=PARAMS,
        cost_estimate=pl.CostEstimate(flops=400 * 1024, bytes_accessed=3_000_000, transcendentals=0),
        name="finish",
    )(
        *[in_vmem(value) for value in (received, before, after, rest)],
        in_hbm(side),
        in_hbm(back),
    )


def pairs(size, offset):
    return [(i, (((i - offset) ^ 1) + offset) % size) for i in range(size)]


def transposed(value, rows, order):
    value = value.reshape(N_TH, rows // 4, 4, LANES)
    value = lax.all_to_all(value, "th", 0, 0, tiled=True, axis_index_groups=[order])
    return value.reshape(N_TH * rows, LANES)


def per_device(density, velocity, pressure):
    high, low = filter_matrices()
    high, low = jnp.asarray(high), jnp.asarray(low)
    table = jnp.asarray(edge_weights())
    sent = inner_part(density, velocity, pressure)
    received = transposed(sent, SEND_ROWS, ORDER)

    near_row, far_row, columns = edges(density, velocity, pressure)
    th_far = lax.ppermute(far_row, "th", pairs(N_TH, 1))
    th_near = lax.ppermute(near_row, "th", pairs(N_TH, 0))

    rest, matrices, weights = outer_part(high, low, table, density, velocity, pressure)
    back, up, down = filtered(received, matrices, weights, columns)
    up, down, th_far, th_near = lax.optimization_barrier((up, down, th_far, th_near))
    returned = transposed(back, BACK_ROWS, BACK_ORDER)
    size = lax.axis_size("gz")
    before = lax.ppermute(up, "gz", [(i, (i + 1) % size) for i in range(size)])
    after = lax.ppermute(down, "gz", [(i, (i - 1) % size) for i in range(size)])
    return finish(returned, before, after, rest, th_near, th_far)


def solution(mesh):
    in_specs = (P("th", None, "gz"), P(None, "th", None, "gz"), P("th", None, "gz"))
    out_specs = P(None, "th", None, "gz")
    return jax.shard_map(
        per_device, mesh=mesh, in_specs=in_specs, out_specs=out_specs, check_vma=False
    )
```

```python
import math

import jax
import jax.numpy as jnp
import ml_dtypes
import numpy as np
from jax import lax
from jax.experimental import pallas as pl
from jax.experimental.pallas import tpu as pltpu
from jax.sharding import PartitionSpec as P

NTH = 256
NR = 64
NF = 8
N_TH = 32
SECTOR = NTH // N_TH
LANES = 128
FIELDS = 5
SEND_ROWS = 20
BACK_ROWS = 12
OUTER = NR - NF
BLOCK_ROWS = FIELDS * SECTOR * OUTER
PACK_ROWS = SECTOR + NR // 2
UP_ROWS, DOWN_ROWS = 0, 0
ORDER = [(23 + n) % N_TH for n in range(N_TH)]
BACK_ORDER = [(16 + n) % N_TH for n in range(N_TH)]
ROW_FIELDS = 11

HALF_STEP = 0.125
SMOOTH = 0.05


def theta_factor(cycle):
    return 0.25 / (2.0 * (2.0 * math.pi / NTH) * (cycle + 0.5))


def filter_rows():
    modes = np.arange(NTH)
    folded = np.minimum(modes, NTH - modes)
    waves = np.cos(2.0 * math.pi * (modes[:, None] * modes[None, :] % NTH) / NTH)
    rows = []
    for cycle in range(NF):
        keep = 2 * (NF + 1) * folded <= NTH * (cycle + 1)
        rows.append(waves[:, keep].sum(axis=1) / NTH)
    return np.stack(rows)


def filter_matrices():
    rows = filter_rows()
    index = (np.arange(NTH)[:, None] - np.arange(NTH)[None, :]) % NTH
    full = np.concatenate([rows[:, index], rows[:1, (index + NTH // 2) % NTH]]).astype(np.float32)
    high = full.astype(ml_dtypes.bfloat16)
    low = (full - high.astype(np.float32)).astype(ml_dtypes.bfloat16)
    return high, low


def edge_weights():
    rows = filter_rows()
    table = np.zeros((2 * N_TH, SECTOR, LANES), np.float32)
    for row in range(2 * N_TH - 1):
        apart = (N_TH - 1 - row) * SECTOR
        index = (apart + np.arange(SECTOR)[:, None] - np.arange(SECTOR)[None, :]) % NTH
        block = np.repeat(rows[:, index].transpose(1, 0, 2)[..., None], 2, axis=3)
        table[row] = block.reshape(SECTOR, LANES)
    return table.reshape(2 * N_TH * SECTOR, LANES)


def conserved(fields):
    rho, ur, ut, uz, p = fields
    qr, qt, qz = rho * ur, rho * ut, rho * uz
    energy = p * 2.5 + 0.5 * (qr * ur + qt * ut + qz * uz)
    return rho, qr, qt, qz, energy


def flux(fields, q, direction):
    p = fields[4]
    speed = fields[1 + direction]
    moving = q[1 + direction]
    parts = [moving, moving * fields[1], moving * fields[2], moving * fields[3], speed * (q[4] + p)]
    parts[1 + direction] = parts[1 + direction] + p
    return parts


def slot(sector, order):
    return order.index(sector)


def lanes_of(shape):
    return lax.broadcasted_iota(jnp.int32, shape, len(shape) - 1)


def rows_of(shape):
    return lax.broadcasted_iota(jnp.int32, shape, len(shape) - 2)


def spread(value, shift, axis):
    size = value.shape[axis]
    return pltpu.roll(value, shift % size, axis)


def half_packs(tile):
    turned = spread(tile, 64, 1)
    low = lanes_of((SECTOR, LANES)) < 64
    first = jnp.where(low, tile, spread(turned, 4, 0))
    second = jnp.where(low, turned, spread(tile, 4, 0))
    return first[:4], second[:4]


def inner_kernel(d_ref, u_ref, w_ref, v_ref, p_ref, out_ref):
    flat = [ref.reshape(16 * SECTOR, LANES) for ref in (d_ref, u_ref, w_ref, v_ref, p_ref)]

    def load(cycle):
        return [ref[pl.ds(cycle, SECTOR, stride=16), :] for ref in flat]

    def store(unit, row, value):
        start = slot(unit, ORDER) * SEND_ROWS + row
        out_ref[start : start + value.shape[0], :] = value

    shape = (SECTOR, LANES)
    lane, row = lanes_of(shape), rows_of(shape)
    first_lane, last_lane = lane == 0, lane == LANES - 1
    not_first_row, not_last_row = row > 0, row < SECTOR - 1
    low = lanes_of((1, LANES)) < 64
    for unit in range(16, N_TH):
        store(unit, 9, jnp.zeros((5, LANES), jnp.float32))

    before = None
    fields = load(0)
    q = conserved(fields)
    radial = flux(fields, q, 0)
    for f in range(FIELDS):
        sign = -1.0 if f in (1, 2) else 1.0
        mirrored = sign * (SMOOTH * q[f] + HALF_STEP * radial[f])
        for half, pack in enumerate(half_packs(mirrored)):
            store(16 + 2 * f + half, 10, pack)
    border = [jnp.zeros(shape, jnp.float32) for _ in range(FIELDS)]
    for cycle in range(NF):
        after_fields = load(cycle + 1)
        after_q = conserved(after_fields)
        after = (after_q, flux(after_fields, after_q, 0))
        around = flux(fields, q, 1)
        along = flux(fields, q, 2)
        c = theta_factor(cycle)
        radius = cycle + 0.5
        scale = 0.25 / radius
        sources = (
            None,
            scale * (q[2] * fields[2] + fields[4]),
            -scale * (q[1] * fields[2]),
            None,
            None,
        )
        for f in range(FIELDS):
            own = q[f] * (0.8 - 0.8 * c)
            if sources[f] is not None:
                own = own + sources[f]
            smooth, push = SMOOTH * q[f], HALF_STEP * along[f]
            forward, backward = spread(smooth + push, 1, 1), spread(smooth - push, -1, 1)
            own = own + jnp.where(first_lane, 0.0, forward) + jnp.where(last_lane, 0.0, backward)
            beyond = jnp.where(first_lane, forward, jnp.where(last_lane, backward, 0.0))
            border[f] = border[f] + spread(beyond, 16 * cycle + 1, 1)
            smooth, push = (0.4 * c) * q[f], c * around[f]
            rising, falling = smooth + push, smooth - push
            own = own + jnp.where(not_first_row, spread(rising, 1, 0), 0.0)
            own = own + jnp.where(not_last_row, spread(falling, -1, 0), 0.0)
            own = own + (SMOOTH * after[0][f] - (HALF_STEP * (radius + 1.0) / radius) * after[1][f])
            if before is not None:
                own = own + (SMOOTH * before[0][f] + (HALF_STEP * (radius - 1.0) / radius) * before[1][f])
            up, down = rising[7:8], falling[0:1]
            if f < 4:
                unit = f * NF + cycle
                store(unit, 0, own)
                store(unit, 8, up)
                store(unit, 15, down)
            else:
                packs = half_packs(own)
                store(cycle, 10, packs[0])
                store(cycle, 9, jnp.where(low, down, spread(up, 64, 1)))
                store(NF + cycle, 10, packs[1])
                store(NF + cycle, 9, jnp.where(low, spread(down, 64, 1), up))
        before = (q, radial)
        fields, q, radial = after_fields, after_q, after[1]
    rows = [
        jnp.sum(pltpu.roll(value, 0, 1, stride=2, stride_axis=0), axis=0, keepdims=True) for value in border
    ]
    others = jnp.concatenate(rows[1:], axis=0)
    for unit in range(N_TH):
        store(unit, 14, rows[0])
        store(unit, 16, others)


def in_vmem(value):
    return pltpu.with_memory_space_constraint(value, pltpu.VMEM)


def in_hbm(value):
    return pltpu.with_memory_space_constraint(value, pltpu.HBM)


PARAMS = pltpu.CompilerParams(vmem_limit_bytes=24 << 20)
WHOLE = pl.BlockSpec(memory_space=pltpu.VMEM)


def inner_part(density, velocity, pressure):
    return pl.pallas_call(
        inner_kernel,
        grid=(1,),
        in_specs=[
            pl.BlockSpec((SECTOR, 16, LANES), lambda i: (0, 0, 0)),
            *[pl.BlockSpec((None, SECTOR, 16, LANES), lambda i, n=n: (n, 0, 0, 0)) for n in range(3)],
            pl.BlockSpec((SECTOR, 16, LANES), lambda i: (0, 0, 0)),
        ],
        out_specs=WHOLE,
        out_shape=pltpu.VMEM((N_TH * SEND_ROWS, LANES), jnp.float32),
        compiler_params=PARAMS,
        cost_estimate=pl.CostEstimate(flops=8 * 1024 * 200, bytes_accessed=600_000, transcendentals=0),
        name="inner_part",
    )(in_hbm(density), *[in_hbm(velocity)] * 3, in_hbm(pressure))


def edge_kernel(d_ref, v_ref, p_ref, near_ref, far_ref, columns_ref):
    lane = lanes_of((NR, LANES))
    odd = lax.axis_index("th") % 2 == 1

    def load(f, j):
        return d_ref[j] if f == 0 else (p_ref[j] if f == 4 else v_ref[f - 1, j])

    firsts = jnp.zeros((NR, LANES), jnp.float32)
    lasts = firsts
    for f in range(FIELDS):
        for j in range(SECTOR):
            spot = 16 * f + 2 * j
            value = spread(load(f, j), spot + 1, 1)
            firsts = jnp.where(lane == spot + 1, value, firsts)
            lasts = jnp.where(lane == spot, value, lasts)
        first, last = load(f, 0), load(f, SECTOR - 1)
        near_ref[f] = jnp.where(odd, first, last)
        far_ref[f] = jnp.where(odd, last, first)
    columns_ref[...] = spread(firsts, -1, 1) + spread(lasts, 1, 1)


def edges(density, velocity, pressure):
    rows = pltpu.VMEM((ROW_FIELDS, NR, LANES), jnp.float32)
    return pl.pallas_call(
        edge_kernel,
        in_specs=[WHOLE] * 3,
        out_specs=[WHOLE] * 3,
        out_shape=[rows, rows, pltpu.VMEM((NR, LANES), jnp.float32)],
        compiler_params=PARAMS,
        cost_estimate=pl.CostEstimate(flops=320 * 1024 * 3, bytes_accessed=1_800_000, transcendentals=0),
        name="edges",
    )(in_vmem(density), in_vmem(velocity), in_vmem(pressure))


def axial_terms(both):
    lane = lanes_of(both.shape)
    fields = [both] + [spread(both, -16 * f, 1) for f in range(1, FIELDS)]
    q = conserved(fields)
    along = flux(fields, q, 2)
    push = jnp.where(lane % 2 == 1, HALF_STEP, -HALF_STEP)
    return [SMOOTH * q[f] + push * along[f] for f in range(FIELDS)]


def filter_kernel(r_ref, w_ref, weights_ref, columns_ref, out_ref, up_ref, down_ref):
    shape = (N_TH, SECTOR, LANES)
    row, lane = rows_of(shape), lanes_of(shape)
    starts = [slot(s, ORDER) * SEND_ROWS for s in range(N_TH)]
    main = jnp.stack([r_ref[a : a + 8, :] for a in starts])
    extra = jnp.stack([r_ref[a + 8 : a + 16, :] for a in starts])
    zero = jnp.zeros(shape, jnp.float32)

    def earlier(value):
        return jnp.concatenate([value[-1:], value[:-1]], axis=0)

    def later(value):
        return jnp.concatenate([value[1:], value[:1]], axis=0)

    main = main + jnp.where(row == 0, earlier(extra), jnp.where(row == 7, later(extra), zero))
    turned = spread(extra, 64, 2)
    top = spread(extra, 6, 1)
    half = jnp.where(row < 4, top, spread(turned, 2, 1))
    half = half + jnp.where(
        row == 0, earlier(spread(turned, 7, 1)), jnp.where(row == 7, later(top), zero)
    )

    def product(high, low, value):
        value = value.reshape(NTH, LANES)
        big = value.astype(jnp.bfloat16)
        small = (value - big.astype(jnp.float32)).astype(jnp.bfloat16)
        out = jnp.dot(high, big, preferred_element_type=jnp.float32)
        out = out + jnp.dot(high, small, preferred_element_type=jnp.float32)
        out = out + jnp.dot(low, big, preferred_element_type=jnp.float32)
        return out.reshape(shape)

    main = product(w_ref[0], w_ref[1], main)
    half = product(w_ref[2], w_ref[3], half)
    packed = jnp.where(lane < 64, half, spread(spread(half, 64, 2), 4, 1))
    sums = [jnp.zeros((SECTOR, LANES), jnp.float32) for _ in range(FIELDS)]
    for s in range(N_TH):
        base, start = slot(s, BACK_ORDER) * BACK_ROWS, starts[s]
        out_ref[base : base + 8, :] = main[s]
        out_ref[base + 8 : base + 12, :] = packed[s, :4]
        weights = weights_ref[SECTOR * s : SECTOR * (s + 1), :]
        for f, place in enumerate((14, 16, 17, 18, 19)):
            sums[f] = sums[f] + weights * r_ref[start + place : start + place + 1, :]
    first = lanes_of((SECTOR, LANES)) % 16 < 2
    terms = jnp.zeros((SECTOR, LANES), jnp.float32)
    for f in range(FIELDS):
        for shift in (2, 4, 8):
            sums[f] = sums[f] + spread(sums[f], -shift, 1)
        terms = terms + spread(jnp.where(first, sums[f], 0.0), 2 * f, 1)
    columns = columns_ref[...]
    up, down = two_halves(columns[: NR // 2], columns[NR // 2 :])
    for target, value in ((up_ref, up), (down_ref, down)):
        target[:SECTOR, :] = terms
        target[SECTOR:PACK_ROWS, :] = value


def two_halves(upper, lower):
    odd = lanes_of(upper.shape) % 2 == 1
    return jnp.where(odd, upper, spread(lower, -1, 1)), jnp.where(odd, spread(upper, 1, 1), lower)


def from_halves(odd_lanes, even_lanes):
    odd = lanes_of(odd_lanes.shape) % 2 == 1
    upper = jnp.where(odd, odd_lanes, spread(even_lanes, -1, 1))
    lower = jnp.where(odd, spread(odd_lanes, 1, 1), even_lanes)
    return upper, lower


def filtered(received, matrices, weights, columns):
    up = pltpu.VMEM((PACK_ROWS + UP_ROWS, LANES), jnp.float32)
    down = pltpu.VMEM((PACK_ROWS + DOWN_ROWS, LANES), jnp.float32)
    return pl.pallas_call(
        filter_kernel,
        in_specs=[WHOLE] * 4,
        out_specs=[WHOLE] * 3,
        out_shape=[pltpu.VMEM((N_TH * BACK_ROWS, LANES), jnp.float32), up, down],
        compiler_params=PARAMS,
        cost_estimate=pl.CostEstimate(flops=6 * 256 * 256 * 256, bytes_accessed=1_200_000, transcendentals=0),
        name="filtered",
    )(*[in_vmem(value) for value in (received, matrices, weights, columns)])


def theta_terms(fields, q, c):
    around = flux(fields, q, 1)
    smooth = [(0.4 * c) * part for part in q]
    push = [c * part for part in around]
    return [a + b for a, b in zip(smooth, push)], [a - b for a, b in zip(smooth, push)]


def outer_kernel(
    high_ref, low_ref, table_ref, d_ref, v_ref, p_ref, out_ref, w_ref, weights_ref, rising_ref, done
):
    th = lax.axis_index("th")
    cycle = th % NF
    half = jnp.where(th < 2 * NF, cycle, jnp.where(th < 2 * NF + 2 * FIELDS, NF, 0))
    copies = [
        pltpu.make_async_copy(table.at[place], w_ref.at[2 * k + n], done.at[2 * k + n])
        for k, place in enumerate((cycle, half))
        for n, table in enumerate((high_ref, low_ref))
    ]
    first = pl.multiple_of((N_TH - 1 - th) * SECTOR, SECTOR)
    copies.append(
        pltpu.make_async_copy(table_ref.at[pl.ds(first, N_TH * SECTOR), :], weights_ref, done.at[4])
    )
    for copy in copies:
        copy.start()
    shape = (NR, LANES)
    lane, row = lanes_of(shape)[NF:], rows_of(shape)
    radius = row.astype(jnp.float32) + 0.5
    inverse = (1.0 / radius)[NF:]
    c = (theta_factor(0) * 0.5) * inverse
    first_lane, last_lane = lane == 0, lane == LANES - 1
    last_row = row == NR - 1
    own_scale, source_scale = 0.8 - 0.8 * c, 0.25 * inverse
    push_scale = HALF_STEP * radius
    for f in range(FIELDS):
        rising_ref[f] = jnp.zeros((NR - NF, LANES), jnp.float32)

    def rows_at(f, j):
        return pl.ds(pl.multiple_of((f * SECTOR + j) * OUTER, NF), OUTER)

    def step(j, carry):
        every = (d_ref[j], v_ref[0, j], v_ref[1, j], v_ref[2, j], p_ref[j])
        every_q = conserved(every)
        radial = flux(every, every_q, 0)
        fields, q = [part[NF:] for part in every], [part[NF:] for part in every_q]
        along = flux(fields, q, 2)
        rising, falling = theta_terms(fields, q, c)
        sources = (
            None,
            source_scale * (q[2] * fields[2] + fields[4]),
            -source_scale * (q[1] * fields[2]),
            None,
            None,
        )
        for f in range(FIELDS):
            own = q[f] * own_scale
            if sources[f] is not None:
                own = own + sources[f]
            smooth, push = SMOOTH * every_q[f], HALF_STEP * along[f]
            near = smooth[NF:]
            own = own + jnp.where(first_lane, 0.0, spread(near + push, 1, 1))
            own = own + jnp.where(last_lane, 0.0, spread(near - push, LANES - 1, 1))
            push = push_scale * radial[f]
            ghost = push + HALF_STEP * radial[f]
            smooth_ahead = jnp.where(last_row, smooth, spread(smooth, NR - 1, 0))
            push_ahead = jnp.where(last_row, ghost, spread(push, NR - 1, 0))
            own = own + (smooth_ahead + spread(smooth, 1, 0))[NF:]
            own = own + inverse * (spread(push, 1, 0) - push_ahead)[NF:]
            out_ref[rows_at(f, j), :] = own + rising_ref[f]
            rising_ref[f] = rising[f]

        @pl.when(j > 0)
        def _():
            for f in range(FIELDS):
                out_ref[rows_at(f, j - 1), :] = out_ref[rows_at(f, j - 1), :] + falling[f]

        return carry

    lax.fori_loop(0, SECTOR, step, 0)
    for copy in copies:
        copy.wait()


def outer_part(high, low, table, density, velocity, pressure):
    return pl.pallas_call(
        outer_kernel,
        in_specs=[pl.BlockSpec(memory_space=pl.ANY)] * 3 + [WHOLE] * 3,
        out_specs=[WHOLE] * 3,
        out_shape=[
            pltpu.VMEM((BLOCK_ROWS, LANES), jnp.float32),
            pltpu.VMEM((4, NTH, NTH), jnp.bfloat16),
            pltpu.VMEM((N_TH * SECTOR, LANES), jnp.float32),
        ],
        scratch_shapes=[
            pltpu.VMEM((FIELDS, NR - NF, LANES), jnp.float32),
            pltpu.SemaphoreType.DMA((5,)),
        ],
        compiler_params=PARAMS,
        cost_estimate=pl.CostEstimate(flops=64 * 1024 * 250, bytes_accessed=3_000_000, transcendentals=0),
        name="outer_part",
    )(
        *[in_hbm(value) for value in (high, low, table)],
        *[in_vmem(value) for value in (density, velocity, pressure)],
    )


def finish_kernel(
    r_ref, before_ref, after_ref, rest_ref, side_ref, back_ref, out_ref, buffer, rows_ref, done
):
    arrivals = [
        pltpu.make_async_copy(
            value.at[pl.ds(0, FIELDS), pl.ds(NF, NR - NF), :], rows_ref.at[n], done.at[SECTOR + 1 + n]
        )
        for n, value in enumerate((side_ref, back_ref))
    ]
    for copy in arrivals:
        copy.start()
    before, after = before_ref[:PACK_ROWS, :], after_ref[:PACK_ROWS, :]
    upper, lower = from_halves(before[SECTOR:], after[SECTOR:])
    terms = axial_terms(jnp.concatenate([upper, lower], axis=0)[NF:])
    shape = (SECTOR, LANES)
    lane = lanes_of(shape)
    ends = (lane == 0) | (lane == LANES - 1)
    border = jnp.where(lane % 2 == 1, before[:SECTOR], after[:SECTOR])
    low_half = lanes_of((4, LANES)) < 64
    far_lane = lanes_of((NR - NF, LANES))
    far_ends = (far_lane == 0) | (far_lane == LANES - 1)

    def outer(j):
        rows = pl.ds(NF, NR - NF)
        return pltpu.make_async_copy(buffer.at[:, j, rows, :], out_ref.at[:, j, rows, :], done.at[j])

    def write_outer(j, more):
        for f in range(FIELDS):
            beyond = jnp.where(far_ends, spread(terms[f], LANES - 1 - 2 * j, 1), 0.0)
            if more is not None:
                beyond = beyond + more[f]
            first = (f * SECTOR + j) * OUTER
            buffer[f, j, NF:, :] = rest_ref[first : first + OUTER, :] + beyond
        outer(j).start()

    for j in range(1, SECTOR - 1):
        write_outer(j, None)

    tiles = buffer.reshape(FIELDS * SECTOR * NR, LANES)

    def joined(unit_a, unit_b):
        start_a, start_b = (slot(unit, BACK_ORDER) * BACK_ROWS + 8 for unit in (unit_a, unit_b))
        a, b = r_ref[start_a : start_a + 4, :], r_ref[start_b : start_b + 4, :]
        top = jnp.where(low_half, a, spread(b, 64, 1))
        bottom = jnp.where(low_half, spread(a, 64, 1), b)
        return jnp.concatenate([top, bottom], axis=0)

    for f in range(FIELDS):
        for cycle in range(NF):
            if f < 4:
                start = slot(f * NF + cycle, BACK_ORDER) * BACK_ROWS
                tile = r_ref[start : start + 8, :]
            else:
                tile = joined(cycle, NF + cycle)
            if cycle == 0:
                tile = tile + joined(16 + 2 * f, 17 + 2 * f)
            tile = tile + jnp.where(ends, spread(border, -(16 * cycle + 2 * f + 1), 1), 0.0)
            tiles[pl.ds(f * SECTOR * NR + cycle, SECTOR, stride=NR), :] = tile
    rows = pl.ds(0, NF)
    inner = pltpu.make_async_copy(buffer.at[:, :, rows, :], out_ref.at[:, :, rows, :], done.at[SECTOR])
    inner.start()
    for copy in arrivals:
        copy.wait()
    c = (theta_factor(0) * 0.5) / (rows_of((NR, LANES))[NF:].astype(jnp.float32) + 0.5)
    odd = lax.axis_index("th") % 2 == 1
    side = [rows_ref[0, f] for f in range(FIELDS)]
    back = [rows_ref[1, f] for f in range(FIELDS)]
    below = [jnp.where(odd, a, b) for a, b in zip(side, back)]
    above = [jnp.where(odd, b, a) for a, b in zip(side, back)]
    write_outer(0, theta_terms(below, conserved(below), c)[0])
    write_outer(SECTOR - 1, theta_terms(above, conserved(above), c)[1])
    for j in range(SECTOR):
        outer(j).wait()
    inner.wait()


def finish(received, before, after, rest, side, back):
    block = (FIELDS, SECTOR, NR, LANES)
    return pl.pallas_call(
        finish_kernel,
        in_specs=[WHOLE] * 4 + [pl.BlockSpec(memory_space=pl.ANY)] * 2,
        out_specs=pl.BlockSpec(memory_space=pl.ANY),
        out_shape=jax.ShapeDtypeStruct(block, jnp.float32),
        scratch_shapes=[
            pltpu.VMEM(block, jnp.float32),
            pltpu.VMEM((2, FIELDS, NR - NF, LANES), jnp.float32),
            pltpu.SemaphoreType.DMA((SECTOR + 3,)),
        ],
        compiler_params=PARAMS,
        cost_estimate=pl.CostEstimate(flops=400 * 1024, bytes_accessed=3_000_000, transcendentals=0),
        name="finish",
    )(
        *[in_vmem(value) for value in (received, before, after, rest)],
        in_hbm(side),
        in_hbm(back),
    )


def pairs(size, offset):
    return [(i, (((i - offset) ^ 1) + offset) % size) for i in range(size)]


def transposed(value, rows, order):
    value = value.reshape(N_TH, rows // 4, 4, LANES)
    value = lax.all_to_all(value, "th", 0, 0, tiled=True, axis_index_groups=[order])
    return value.reshape(N_TH * rows, LANES)


def per_device(density, velocity, pressure):
    high, low = filter_matrices()
    high, low = jnp.asarray(high), jnp.asarray(low)
    table = jnp.asarray(edge_weights())
    sent = inner_part(density, velocity, pressure)
    received = transposed(sent, SEND_ROWS, ORDER)

    near_row, far_row, columns = edges(density, velocity, pressure)
    th_far = lax.ppermute(far_row, "th", pairs(N_TH, 1))
    th_near = lax.ppermute(near_row, "th", pairs(N_TH, 0))

    rest, matrices, weights = outer_part(high, low, table, density, velocity, pressure)
    back, up, down = filtered(received, matrices, weights, columns)
    up, down, th_far, th_near = lax.optimization_barrier((up, down, th_far, th_near))
    returned = transposed(back, BACK_ROWS, BACK_ORDER)
    size = lax.axis_size("gz")
    before = lax.ppermute(up, "gz", [(i, (i + 1) % size) for i in range(size)])
    after = lax.ppermute(down, "gz", [(i, (i - 1) % size) for i in range(size)])
    return finish(returned, before, after, rest, th_near, th_far)


def solution(mesh):
    in_specs = (P("th", None, "gz"), P(None, "th", None, "gz"), P("th", None, "gz"))
    out_specs = P(None, "th", None, "gz")
    return jax.shard_map(
        per_device, mesh=mesh, in_specs=in_specs, out_specs=out_specs, check_vma=False
    )
```

```python
import math

import jax
import jax.numpy as jnp
import ml_dtypes
import numpy as np
from jax import lax
from jax.experimental import pallas as pl
from jax.experimental.pallas import tpu as pltpu
from jax.sharding import PartitionSpec as P

NTH = 256
NR = 64
NF = 8
N_TH = 32
SECTOR = NTH // N_TH
LANES = 128
FIELDS = 5
SEND_ROWS = 20
BACK_ROWS = 12
OUTER = NR - NF
BLOCK_ROWS = FIELDS * SECTOR * OUTER
PACK_ROWS = SECTOR + NR // 2
UP_ROWS, DOWN_ROWS = 0, 0
ORDER = [(23 + n) % N_TH for n in range(N_TH)]
BACK_ORDER = [(18 + n) % N_TH for n in range(N_TH)]
ROW_FIELDS = 11

HALF_STEP = 0.125
SMOOTH = 0.05


def theta_factor(cycle):
    return 0.25 / (2.0 * (2.0 * math.pi / NTH) * (cycle + 0.5))


def filter_rows():
    modes = np.arange(NTH)
    folded = np.minimum(modes, NTH - modes)
    waves = np.cos(2.0 * math.pi * (modes[:, None] * modes[None, :] % NTH) / NTH)
    rows = []
    for cycle in range(NF):
        keep = 2 * (NF + 1) * folded <= NTH * (cycle + 1)
        rows.append(waves[:, keep].sum(axis=1) / NTH)
    return np.stack(rows)


def filter_matrices():
    rows = filter_rows()
    index = (np.arange(NTH)[:, None] - np.arange(NTH)[None, :]) % NTH
    full = np.concatenate([rows[:, index], rows[:1, (index + NTH // 2) % NTH]]).astype(np.float32)
    high = full.astype(ml_dtypes.bfloat16)
    low = (full - high.astype(np.float32)).astype(ml_dtypes.bfloat16)
    return high, low


def edge_weights():
    rows = filter_rows()
    table = np.zeros((2 * N_TH, SECTOR, LANES), np.float32)
    for row in range(2 * N_TH - 1):
        apart = (N_TH - 1 - row) * SECTOR
        index = (apart + np.arange(SECTOR)[:, None] - np.arange(SECTOR)[None, :]) % NTH
        block = np.repeat(rows[:, index].transpose(1, 0, 2)[..., None], 2, axis=3)
        table[row] = block.reshape(SECTOR, LANES)
    return table.reshape(2 * N_TH * SECTOR, LANES)


def conserved(fields):
    rho, ur, ut, uz, p = fields
    qr, qt, qz = rho * ur, rho * ut, rho * uz
    energy = p * 2.5 + 0.5 * (qr * ur + qt * ut + qz * uz)
    return rho, qr, qt, qz, energy


def flux(fields, q, direction):
    p = fields[4]
    speed = fields[1 + direction]
    moving = q[1 + direction]
    parts = [moving, moving * fields[1], moving * fields[2], moving * fields[3], speed * (q[4] + p)]
    parts[1 + direction] = parts[1 + direction] + p
    return parts


def slot(sector, order):
    return order.index(sector)


def lanes_of(shape):
    return lax.broadcasted_iota(jnp.int32, shape, len(shape) - 1)


def rows_of(shape):
    return lax.broadcasted_iota(jnp.int32, shape, len(shape) - 2)


def spread(value, shift, axis):
    size = value.shape[axis]
    return pltpu.roll(value, shift % size, axis)


def half_packs(tile):
    turned = spread(tile, 64, 1)
    low = lanes_of((SECTOR, LANES)) < 64
    first = jnp.where(low, tile, spread(turned, 4, 0))
    second = jnp.where(low, turned, spread(tile, 4, 0))
    return first[:4], second[:4]


def inner_kernel(d_ref, u_ref, w_ref, v_ref, p_ref, out_ref):
    flat = [ref.reshape(16 * SECTOR, LANES) for ref in (d_ref, u_ref, w_ref, v_ref, p_ref)]

    def load(cycle):
        return [ref[pl.ds(cycle, SECTOR, stride=16), :] for ref in flat]

    def store(unit, row, value):
        start = slot(unit, ORDER) * SEND_ROWS + row
        out_ref[start : start + value.shape[0], :] = value

    shape = (SECTOR, LANES)
    lane, row = lanes_of(shape), rows_of(shape)
    first_lane, last_lane = lane == 0, lane == LANES - 1
    not_first_row, not_last_row = row > 0, row < SECTOR - 1
    low = lanes_of((1, LANES)) < 64
    for unit in range(16, N_TH):
        store(unit, 9, jnp.zeros((5, LANES), jnp.float32))

    before = None
    fields = load(0)
    q = conserved(fields)
    radial = flux(fields, q, 0)
    for f in range(FIELDS):
        sign = -1.0 if f in (1, 2) else 1.0
        mirrored = sign * (SMOOTH * q[f] + HALF_STEP * radial[f])
        for half, pack in enumerate(half_packs(mirrored)):
            store(16 + 2 * f + half, 10, pack)
    border = [jnp.zeros(shape, jnp.float32) for _ in range(FIELDS)]
    for cycle in range(NF):
        after_fields = load(cycle + 1)
        after_q = conserved(after_fields)
        after = (after_q, flux(after_fields, after_q, 0))
        around = flux(fields, q, 1)
        along = flux(fields, q, 2)
        c = theta_factor(cycle)
        radius = cycle + 0.5
        scale = 0.25 / radius
        sources = (
            None,
            scale * (q[2] * fields[2] + fields[4]),
            -scale * (q[1] * fields[2]),
            None,
            None,
        )
        for f in range(FIELDS):
            own = q[f] * (0.8 - 0.8 * c)
            if sources[f] is not None:
                own = own + sources[f]
            smooth, push = SMOOTH * q[f], HALF_STEP * along[f]
            forward, backward = spread(smooth + push, 1, 1), spread(smooth - push, -1, 1)
            own = own + jnp.where(first_lane, 0.0, forward) + jnp.where(last_lane, 0.0, backward)
            beyond = jnp.where(first_lane, forward, jnp.where(last_lane, backward, 0.0))
            border[f] = border[f] + spread(beyond, 16 * cycle + 1, 1)
            smooth, push = (0.4 * c) * q[f], c * around[f]
            rising, falling = smooth + push, smooth - push
            own = own + jnp.where(not_first_row, spread(rising, 1, 0), 0.0)
            own = own + jnp.where(not_last_row, spread(falling, -1, 0), 0.0)
            own = own + (SMOOTH * after[0][f] - (HALF_STEP * (radius + 1.0) / radius) * after[1][f])
            if before is not None:
                own = own + (SMOOTH * before[0][f] + (HALF_STEP * (radius - 1.0) / radius) * before[1][f])
            up, down = rising[7:8], falling[0:1]
            if f < 4:
                unit = f * NF + cycle
                store(unit, 0, own)
                store(unit, 8, up)
                store(unit, 15, down)
            else:
                packs = half_packs(own)
                store(cycle, 10, packs[0])
                store(cycle, 9, jnp.where(low, down, spread(up, 64, 1)))
                store(NF + cycle, 10, packs[1])
                store(NF + cycle, 9, jnp.where(low, spread(down, 64, 1), up))
        before = (q, radial)
        fields, q, radial = after_fields, after_q, after[1]
    rows = [
        jnp.sum(pltpu.roll(value, 0, 1, stride=2, stride_axis=0), axis=0, keepdims=True) for value in border
    ]
    others = jnp.concatenate(rows[1:], axis=0)
    for unit in range(N_TH):
        store(unit, 14, rows[0])
        store(unit, 16, others)


def in_vmem(value):
    return pltpu.with_memory_space_constraint(value, pltpu.VMEM)


def in_hbm(value):
    return pltpu.with_memory_space_constraint(value, pltpu.HBM)


PARAMS = pltpu.CompilerParams(vmem_limit_bytes=24 << 20)
WHOLE = pl.BlockSpec(memory_space=pltpu.VMEM)


def inner_part(density, velocity, pressure):
    return pl.pallas_call(
        inner_kernel,
        grid=(1,),
        in_specs=[
            pl.BlockSpec((SECTOR, 16, LANES), lambda i: (0, 0, 0)),
            *[pl.BlockSpec((None, SECTOR, 16, LANES), lambda i, n=n: (n, 0, 0, 0)) for n in range(3)],
            pl.BlockSpec((SECTOR, 16, LANES), lambda i: (0, 0, 0)),
        ],
        out_specs=WHOLE,
        out_shape=pltpu.VMEM((N_TH * SEND_ROWS, LANES), jnp.float32),
        compiler_params=PARAMS,
        cost_estimate=pl.CostEstimate(flops=8 * 1024 * 200, bytes_accessed=600_000, transcendentals=0),
        name="inner_part",
    )(in_hbm(density), *[in_hbm(velocity)] * 3, in_hbm(pressure))


def edge_kernel(d_ref, v_ref, p_ref, near_ref, far_ref, columns_ref):
    lane = lanes_of((NR, LANES))
    odd = lax.axis_index("th") % 2 == 1

    def load(f, j):
        return d_ref[j] if f == 0 else (p_ref[j] if f == 4 else v_ref[f - 1, j])

    firsts = jnp.zeros((NR, LANES), jnp.float32)
    lasts = firsts
    for f in range(FIELDS):
        for j in range(SECTOR):
            spot = 16 * f + 2 * j
            value = spread(load(f, j), spot + 1, 1)
            firsts = jnp.where(lane == spot + 1, value, firsts)
            lasts = jnp.where(lane == spot, value, lasts)
        first, last = load(f, 0), load(f, SECTOR - 1)
        near_ref[f] = jnp.where(odd, first, last)
        far_ref[f] = jnp.where(odd, last, first)
    columns_ref[...] = spread(firsts, -1, 1) + spread(lasts, 1, 1)


def edges(density, velocity, pressure):
    rows = pltpu.VMEM((ROW_FIELDS, NR, LANES), jnp.float32)
    return pl.pallas_call(
        edge_kernel,
        in_specs=[WHOLE] * 3,
        out_specs=[WHOLE] * 3,
        out_shape=[rows, rows, pltpu.VMEM((NR, LANES), jnp.float32)],
        compiler_params=PARAMS,
        cost_estimate=pl.CostEstimate(flops=320 * 1024 * 3, bytes_accessed=1_800_000, transcendentals=0),
        name="edges",
    )(in_vmem(density), in_vmem(velocity), in_vmem(pressure))


def axial_terms(both):
    lane = lanes_of(both.shape)
    fields = [both] + [spread(both, -16 * f, 1) for f in range(1, FIELDS)]
    q = conserved(fields)
    along = flux(fields, q, 2)
    push = jnp.where(lane % 2 == 1, HALF_STEP, -HALF_STEP)
    return [SMOOTH * q[f] + push * along[f] for f in range(FIELDS)]


def filter_kernel(r_ref, w_ref, weights_ref, columns_ref, out_ref, up_ref, down_ref):
    shape = (N_TH, SECTOR, LANES)
    row, lane = rows_of(shape), lanes_of(shape)
    starts = [slot(s, ORDER) * SEND_ROWS for s in range(N_TH)]
    main = jnp.stack([r_ref[a : a + 8, :] for a in starts])
    extra = jnp.stack([r_ref[a + 8 : a + 16, :] for a in starts])
    zero = jnp.zeros(shape, jnp.float32)

    def earlier(value):
        return jnp.concatenate([value[-1:], value[:-1]], axis=0)

    def later(value):
        return jnp.concatenate([value[1:], value[:1]], axis=0)

    main = main + jnp.where(row == 0, earlier(extra), jnp.where(row == 7, later(extra), zero))
    turned = spread(extra, 64, 2)
    top = spread(extra, 6, 1)
    half = jnp.where(row < 4, top, spread(turned, 2, 1))
    half = half + jnp.where(
        row == 0, earlier(spread(turned, 7, 1)), jnp.where(row == 7, later(top), zero)
    )

    def product(high, low, value):
        value = value.reshape(NTH, LANES)
        big = value.astype(jnp.bfloat16)
        small = (value - big.astype(jnp.float32)).astype(jnp.bfloat16)
        out = jnp.dot(high, big, preferred_element_type=jnp.float32)
        out = out + jnp.dot(high, small, preferred_element_type=jnp.float32)
        out = out + jnp.dot(low, big, preferred_element_type=jnp.float32)
        return out.reshape(shape)

    main = product(w_ref[0], w_ref[1], main)
    half = product(w_ref[2], w_ref[3], half)
    packed = jnp.where(lane < 64, half, spread(spread(half, 64, 2), 4, 1))
    sums = [jnp.zeros((SECTOR, LANES), jnp.float32) for _ in range(FIELDS)]
    for s in range(N_TH):
        base, start = slot(s, BACK_ORDER) * BACK_ROWS, starts[s]
        out_ref[base : base + 8, :] = main[s]
        out_ref[base + 8 : base + 12, :] = packed[s, :4]
        weights = weights_ref[SECTOR * s : SECTOR * (s + 1), :]
        for f, place in enumerate((14, 16, 17, 18, 19)):
            sums[f] = sums[f] + weights * r_ref[start + place : start + place + 1, :]
    first = lanes_of((SECTOR, LANES)) % 16 < 2
    terms = jnp.zeros((SECTOR, LANES), jnp.float32)
    for f in range(FIELDS):
        for shift in (2, 4, 8):
            sums[f] = sums[f] + spread(sums[f], -shift, 1)
        terms = terms + spread(jnp.where(first, sums[f], 0.0), 2 * f, 1)
    columns = columns_ref[...]
    up, down = two_halves(columns[: NR // 2], columns[NR // 2 :])
    for target, value in ((up_ref, up), (down_ref, down)):
        target[:SECTOR, :] = terms
        target[SECTOR:PACK_ROWS, :] = value


def two_halves(upper, lower):
    odd = lanes_of(upper.shape) % 2 == 1
    return jnp.where(odd, upper, spread(lower, -1, 1)), jnp.where(odd, spread(upper, 1, 1), lower)


def from_halves(odd_lanes, even_lanes):
    odd = lanes_of(odd_lanes.shape) % 2 == 1
    upper = jnp.where(odd, odd_lanes, spread(even_lanes, -1, 1))
    lower = jnp.where(odd, spread(odd_lanes, 1, 1), even_lanes)
    return upper, lower


def filtered(received, matrices, weights, columns):
    up = pltpu.VMEM((PACK_ROWS + UP_ROWS, LANES), jnp.float32)
    down = pltpu.VMEM((PACK_ROWS + DOWN_ROWS, LANES), jnp.float32)
    return pl.pallas_call(
        filter_kernel,
        in_specs=[WHOLE] * 4,
        out_specs=[WHOLE] * 3,
        out_shape=[pltpu.VMEM((N_TH * BACK_ROWS, LANES), jnp.float32), up, down],
        compiler_params=PARAMS,
        cost_estimate=pl.CostEstimate(flops=6 * 256 * 256 * 256, bytes_accessed=1_200_000, transcendentals=0),
        name="filtered",
    )(*[in_vmem(value) for value in (received, matrices, weights, columns)])


def theta_terms(fields, q, c):
    around = flux(fields, q, 1)
    smooth = [(0.4 * c) * part for part in q]
    push = [c * part for part in around]
    return [a + b for a, b in zip(smooth, push)], [a - b for a, b in zip(smooth, push)]


def outer_kernel(
    high_ref, low_ref, table_ref, d_ref, v_ref, p_ref, out_ref, w_ref, weights_ref, rising_ref, done
):
    th = lax.axis_index("th")
    cycle = th % NF
    half = jnp.where(th < 2 * NF, cycle, jnp.where(th < 2 * NF + 2 * FIELDS, NF, 0))
    copies = [
        pltpu.make_async_copy(table.at[place], w_ref.at[2 * k + n], done.at[2 * k + n])
        for k, place in enumerate((cycle, half))
        for n, table in enumerate((high_ref, low_ref))
    ]
    first = pl.multiple_of((N_TH - 1 - th) * SECTOR, SECTOR)
    copies.append(
        pltpu.make_async_copy(table_ref.at[pl.ds(first, N_TH * SECTOR), :], weights_ref, done.at[4])
    )
    for copy in copies:
        copy.start()
    shape = (NR, LANES)
    lane, row = lanes_of(shape)[NF:], rows_of(shape)
    radius = row.astype(jnp.float32) + 0.5
    inverse = (1.0 / radius)[NF:]
    c = (theta_factor(0) * 0.5) * inverse
    first_lane, last_lane = lane == 0, lane == LANES - 1
    last_row = row == NR - 1
    own_scale, source_scale = 0.8 - 0.8 * c, 0.25 * inverse
    push_scale = HALF_STEP * radius
    for f in range(FIELDS):
        rising_ref[f] = jnp.zeros((NR - NF, LANES), jnp.float32)

    def rows_at(f, j):
        return pl.ds(pl.multiple_of((f * SECTOR + j) * OUTER, NF), OUTER)

    def step(j, carry):
        every = (d_ref[j], v_ref[0, j], v_ref[1, j], v_ref[2, j], p_ref[j])
        every_q = conserved(every)
        radial = flux(every, every_q, 0)
        fields, q = [part[NF:] for part in every], [part[NF:] for part in every_q]
        along = flux(fields, q, 2)
        rising, falling = theta_terms(fields, q, c)
        sources = (
            None,
            source_scale * (q[2] * fields[2] + fields[4]),
            -source_scale * (q[1] * fields[2]),
            None,
            None,
        )
        for f in range(FIELDS):
            own = q[f] * own_scale
            if sources[f] is not None:
                own = own + sources[f]
            smooth, push = SMOOTH * every_q[f], HALF_STEP * along[f]
            near = smooth[NF:]
            own = own + jnp.where(first_lane, 0.0, spread(near + push, 1, 1))
            own = own + jnp.where(last_lane, 0.0, spread(near - push, LANES - 1, 1))
            push = push_scale * radial[f]
            ghost = push + HALF_STEP * radial[f]
            smooth_ahead = jnp.where(last_row, smooth, spread(smooth, NR - 1, 0))
            push_ahead = jnp.where(last_row, ghost, spread(push, NR - 1, 0))
            own = own + (smooth_ahead + spread(smooth, 1, 0))[NF:]
            own = own + inverse * (spread(push, 1, 0) - push_ahead)[NF:]
            out_ref[rows_at(f, j), :] = own + rising_ref[f]
            rising_ref[f] = rising[f]

        @pl.when(j > 0)
        def _():
            for f in range(FIELDS):
                out_ref[rows_at(f, j - 1), :] = out_ref[rows_at(f, j - 1), :] + falling[f]

        return carry

    lax.fori_loop(0, SECTOR, step, 0)
    for copy in copies:
        copy.wait()


def outer_part(high, low, table, density, velocity, pressure):
    return pl.pallas_call(
        outer_kernel,
        in_specs=[pl.BlockSpec(memory_space=pl.ANY)] * 3 + [WHOLE] * 3,
        out_specs=[WHOLE] * 3,
        out_shape=[
            pltpu.VMEM((BLOCK_ROWS, LANES), jnp.float32),
            pltpu.VMEM((4, NTH, NTH), jnp.bfloat16),
            pltpu.VMEM((N_TH * SECTOR, LANES), jnp.float32),
        ],
        scratch_shapes=[
            pltpu.VMEM((FIELDS, NR - NF, LANES), jnp.float32),
            pltpu.SemaphoreType.DMA((5,)),
        ],
        compiler_params=PARAMS,
        cost_estimate=pl.CostEstimate(flops=64 * 1024 * 250, bytes_accessed=3_000_000, transcendentals=0),
        name="outer_part",
    )(
        *[in_hbm(value) for value in (high, low, table)],
        *[in_vmem(value) for value in (density, velocity, pressure)],
    )


def finish_kernel(
    r_ref, before_ref, after_ref, rest_ref, side_ref, back_ref, out_ref, buffer, rows_ref, done
):
    arrivals = [
        pltpu.make_async_copy(
            value.at[pl.ds(0, FIELDS), pl.ds(NF, NR - NF), :], rows_ref.at[n], done.at[SECTOR + 1 + n]
        )
        for n, value in enumerate((side_ref, back_ref))
    ]
    for copy in arrivals:
        copy.start()
    before, after = before_ref[:PACK_ROWS, :], after_ref[:PACK_ROWS, :]
    upper, lower = from_halves(before[SECTOR:], after[SECTOR:])
    terms = axial_terms(jnp.concatenate([upper, lower], axis=0)[NF:])
    shape = (SECTOR, LANES)
    lane = lanes_of(shape)
    ends = (lane == 0) | (lane == LANES - 1)
    border = jnp.where(lane % 2 == 1, before[:SECTOR], after[:SECTOR])
    low_half = lanes_of((4, LANES)) < 64
    far_lane = lanes_of((NR - NF, LANES))
    far_ends = (far_lane == 0) | (far_lane == LANES - 1)

    def outer(j):
        rows = pl.ds(NF, NR - NF)
        return pltpu.make_async_copy(buffer.at[:, j, rows, :], out_ref.at[:, j, rows, :], done.at[j])

    def write_outer(j, more):
        for f in range(FIELDS):
            beyond = jnp.where(far_ends, spread(terms[f], LANES - 1 - 2 * j, 1), 0.0)
            if more is not None:
                beyond = beyond + more[f]
            first = (f * SECTOR + j) * OUTER
            buffer[f, j, NF:, :] = rest_ref[first : first + OUTER, :] + beyond
        outer(j).start()

    for j in range(1, SECTOR - 1):
        write_outer(j, None)

    tiles = buffer.reshape(FIELDS * SECTOR * NR, LANES)

    def joined(unit_a, unit_b):
        start_a, start_b = (slot(unit, BACK_ORDER) * BACK_ROWS + 8 for unit in (unit_a, unit_b))
        a, b = r_ref[start_a : start_a + 4, :], r_ref[start_b : start_b + 4, :]
        top = jnp.where(low_half, a, spread(b, 64, 1))
        bottom = jnp.where(low_half, spread(a, 64, 1), b)
        return jnp.concatenate([top, bottom], axis=0)

    for f in range(FIELDS):
        for cycle in range(NF):
            if f < 4:
                start = slot(f * NF + cycle, BACK_ORDER) * BACK_ROWS
                tile = r_ref[start : start + 8, :]
            else:
                tile = joined(cycle, NF + cycle)
            if cycle == 0:
                tile = tile + joined(16 + 2 * f, 17 + 2 * f)
            tile = tile + jnp.where(ends, spread(border, -(16 * cycle + 2 * f + 1), 1), 0.0)
            tiles[pl.ds(f * SECTOR * NR + cycle, SECTOR, stride=NR), :] = tile
    rows = pl.ds(0, NF)
    inner = pltpu.make_async_copy(buffer.at[:, :, rows, :], out_ref.at[:, :, rows, :], done.at[SECTOR])
    inner.start()
    for copy in arrivals:
        copy.wait()
    c = (theta_factor(0) * 0.5) / (rows_of((NR, LANES))[NF:].astype(jnp.float32) + 0.5)
    odd = lax.axis_index("th") % 2 == 1
    side = [rows_ref[0, f] for f in range(FIELDS)]
    back = [rows_ref[1, f] for f in range(FIELDS)]
    below = [jnp.where(odd, a, b) for a, b in zip(side, back)]
    above = [jnp.where(odd, b, a) for a, b in zip(side, back)]
    write_outer(0, theta_terms(below, conserved(below), c)[0])
    write_outer(SECTOR - 1, theta_terms(above, conserved(above), c)[1])
    for j in range(SECTOR):
        outer(j).wait()
    inner.wait()


def finish(received, before, after, rest, side, back):
    block = (FIELDS, SECTOR, NR, LANES)
    return pl.pallas_call(
        finish_kernel,
        in_specs=[WHOLE] * 4 + [pl.BlockSpec(memory_space=pl.ANY)] * 2,
        out_specs=pl.BlockSpec(memory_space=pl.ANY),
        out_shape=jax.ShapeDtypeStruct(block, jnp.float32),
        scratch_shapes=[
            pltpu.VMEM(block, jnp.float32),
            pltpu.VMEM((2, FIELDS, NR - NF, LANES), jnp.float32),
            pltpu.SemaphoreType.DMA((SECTOR + 3,)),
        ],
        compiler_params=PARAMS,
        cost_estimate=pl.CostEstimate(flops=400 * 1024, bytes_accessed=3_000_000, transcendentals=0),
        name="finish",
    )(
        *[in_vmem(value) for value in (received, before, after, rest)],
        in_hbm(side),
        in_hbm(back),
    )


def pairs(size, offset):
    return [(i, (((i - offset) ^ 1) + offset) % size) for i in range(size)]


def transposed(value, rows, order):
    value = value.reshape(N_TH, rows // 4, 4, LANES)
    value = lax.all_to_all(value, "th", 0, 0, tiled=True, axis_index_groups=[order])
    return value.reshape(N_TH * rows, LANES)


def per_device(density, velocity, pressure):
    high, low = filter_matrices()
    high, low = jnp.asarray(high), jnp.asarray(low)
    table = jnp.asarray(edge_weights())
    sent = inner_part(density, velocity, pressure)
    received = transposed(sent, SEND_ROWS, ORDER)

    near_row, far_row, columns = edges(density, velocity, pressure)
    th_far = lax.ppermute(far_row, "th", pairs(N_TH, 1))
    th_near = lax.ppermute(near_row, "th", pairs(N_TH, 0))

    rest, matrices, weights = outer_part(high, low, table, density, velocity, pressure)
    back, up, down = filtered(received, matrices, weights, columns)
    up, down, th_far, th_near = lax.optimization_barrier((up, down, th_far, th_near))
    returned = transposed(back, BACK_ROWS, BACK_ORDER)
    size = lax.axis_size("gz")
    before = lax.ppermute(up, "gz", [(i, (i + 1) % size) for i in range(size)])
    after = lax.ppermute(down, "gz", [(i, (i - 1) % size) for i in range(size)])
    return finish(returned, before, after, rest, th_near, th_far)


def solution(mesh):
    in_specs = (P("th", None, "gz"), P(None, "th", None, "gz"), P("th", None, "gz"))
    out_specs = P(None, "th", None, "gz")
    return jax.shard_map(
        per_device, mesh=mesh, in_specs=in_specs, out_specs=out_specs, check_vma=False
    )
```
